32 devices in a mesh: dp: 16 (over z, x, core), seq: 2 (over y).
Axes of the slice: x: 2, y: 2, z: 4, core: 2. Of those that a mesh axis runs over, the one named last changes fastest.
Arguments:
- latents: bfloat16 [16, 1024, 1152], P('dp', 'seq'), may hold values from -6 to 6
- conditions: float32 [16, 1152], P('dp'), may hold values from -6 to 6
- cotangent: bfloat16 [16, 1024, 1152], P('dp', 'seq'), may hold values from -6 to 6
- qkv_weight: float32 [3981312], P(('dp', 'seq')), may hold values from -0.1875 to 0.1875
- proj_weight: float32 [1327104], P(('dp', 'seq')), may hold values from -0.375 to 0.375
- fc1_weight: float32 [5308416], P(('dp', 'seq')), may hold values from -0.1875 to 0.1875
- fc2_weight: float32 [5308416], P(('dp', 'seq')), may hold values from -0.09375 to 0.09375
- ada_weight: float32 [6912, 1152], P(('dp', 'seq')), may hold values from -0.1875 to 0.1875
- biases: float32 [16128], P(('dp', 'seq')), may hold values from -1.75 to 1.75
- qkv_first: float32 [3981312], P(('dp', 'seq')), may hold values from -40 to 40
- proj_first: float32 [1327104], P(('dp', 'seq')), may hold values from -8 to 8
- fc1_first: float32 [5308416], P(('dp', 'seq')), may hold values from -40 to 40
- fc2_first: float32 [5308416], P(('dp', 'seq')), may hold values from -40 to 40
- ada_first: float32 [6912, 1152], P(('dp', 'seq')), may hold values from -40 to 40
- bias_first: float32 [16128], P(('dp', 'seq')), may hold values from -64 to 64
- qkv_second: float32 [3981312], P(('dp', 'seq')), may hold values from 4.096 to 16.384
- proj_second: float32 [1327104], P(('dp', 'seq')), may hold values from 0.16384 to 0.65536
- fc1_second: float32 [5308416], P(('dp', 'seq')), may hold values from 4.096 to 16.384
- fc2_second: float32 [5308416], P(('dp', 'seq')), may hold values from 4.096 to 16.384
- ada_second: float32 [6912, 1152], P(('dp', 'seq')), may hold values from 4.096 to 16.384
- bias_second: float32 [16128], P(('dp', 'seq')), may hold values from 8.02816 to 32.11264
Outputs:
- block_out: bfloat16 [16, 1024, 1152], P('dp', 'seq')
- input_grad: float32 [16, 1024, 1152], P('dp', 'seq')
- cond_grad: float32 [16, 1152], P('dp')
- new_qkv: float32 [3981312], P(('dp', 'seq'))
- new_proj: float32 [1327104], P(('dp', 'seq'))
- new_fc1: float32 [5308416], P(('dp', 'seq'))
- new_fc2: float32 [5308416], P(('dp', 'seq'))
- new_ada: float32 [6912, 1152], P(('dp', 'seq'))
- new_biases: float32 [16128], P(('dp', 'seq'))
- qkv_first_out: float32 [3981312], P(('dp', 'seq'))
- proj_first_out: float32 [1327104], P(('dp', 'seq'))
- fc1_first_out: float32 [5308416], P(('dp', 'seq'))
- fc2_first_out: float32 [5308416], P(('dp', 'seq'))
- ada_first_out: float32 [6912, 1152], P(('dp', 'seq'))
- bias_first_out: float32 [16128], P(('dp', 'seq'))
- qkv_second_out: float32 [3981312], P(('dp', 'seq'))
- proj_second_out: float32 [1327104], P(('dp', 'seq'))
- fc1_second_out: float32 [5308416], P(('dp', 'seq'))
- fc2_second_out: float32 [5308416], P(('dp', 'seq'))
- ada_second_out: float32 [6912, 1152], P(('dp', 'seq'))
- bias_second_out: float32 [16128], P(('dp', 'seq'))
The draws below stay inside these ranges and needn't reach their ends.
All inputs are finite; a program needn't handle non-finite values.
Results may differ from the reference program's by a relative error of at most 0.01505.
The reference program's roundings to bfloat16 on the way count: a program that leaves them out, or rounds other values in their place, can miss the bound.
Values may be sent and summed in bfloat16 or wider, within the bound.
No kernel may reach another device: no remote copies, remote signals or barrier semaphores. Data moves between devices by JAX's collectives and lax.ppermute only.
A program may use at most 320 MiB of HBM per device.

```python
import math
from functools import partial
import jax
import jax.numpy as jnp
from jax import lax

D = 1152
HEADS = 16
HD = 72
MLP = 4608
TOK_MIN = 1024
STEP = 10
SIXD = 6912
NB = 16128
LAT = 16
LEN = 1024


def shard_levels(key, dims, shards, smallest, high):
    loudness = 1.0
    for dim, shards_of in shards:
        heights = jax.random.uniform(jax.random.fold_in(jax.random.fold_in(key, 6), dim), (shards_of,), jnp.float32, smallest / len(shards), high / len(shards))
        loudness = loudness * jnp.repeat(jnp.exp(heights), dims[dim] // shards_of).reshape((-1,) + (1,) * (len(dims) - 1 - dim))
    return loudness


def noise(stream_key, dims, width, most, pieces=(), dtype=jnp.bfloat16):
    values = jax.random.normal(stream_key, dims, jnp.float32) * width
    if len(pieces) > 0:
        values = shard_levels(stream_key, dims, pieces, -0.22, 0.18) * values
    return jnp.clip(values, min=-most, max=most).astype(dtype)


def setup_inputs(seed: int = 0) -> dict:
    seeds = jax.random.split(jax.random.key(seed), 22)
    return {
        "latents": noise(seeds[0], (LAT, LEN, D), 1.0, 6.0, ((0, 16), (1, 2))),
        "conditions": noise(seeds[1], (LAT, D), 1.0, 6.0, ((0, 16),), jnp.float32),
        "cotangent": noise(seeds[2], (LAT, LEN, D), 1.0, 6.0, ((0, 16), (1, 2))),
        "qkv_weight": noise(seeds[3], (3 * D * D,), D ** -0.5, 0.1875, ((0, 32),), jnp.float32),
        "proj_weight": noise(seeds[4], (D * D,), (max(1, D * 256 // TOK_MIN)) ** -0.5, 0.375, ((0, 32),), jnp.float32),
        "fc1_weight": noise(seeds[5], (D * MLP,), D ** -0.5, 0.1875, ((0, 32),), jnp.float32),
        "fc2_weight": noise(seeds[6], (MLP * D,), MLP ** -0.5, 0.09375, ((0, 32),), jnp.float32),
        "ada_weight": noise(seeds[7], (SIXD, D), D ** -0.5, 0.1875, ((0, 32),), jnp.float32),
        "biases": noise(seeds[8], (NB,), 0.3, 1.75, ((0, 32),), jnp.float32),
        "qkv_first": noise(seeds[9], (3 * D * D,), (0.055 * (LAT * LEN) ** 0.5), 40.0, ((0, 32),), jnp.float32),
        "proj_first": noise(seeds[10], (D * D,), (0.011 * (LAT * LEN) ** 0.5), 8.0, ((0, 32),), jnp.float32),
        "fc1_first": noise(seeds[11], (D * MLP,), (0.055 * (LAT * LEN) ** 0.5), 40.0, ((0, 32),), jnp.float32),
        "fc2_first": noise(seeds[12], (MLP * D,), (0.055 * (LAT * LEN) ** 0.5), 40.0, ((0, 32),), jnp.float32),
        "ada_first": noise(seeds[13], (SIXD, D), (0.055 * (LAT * LEN) ** 0.5), 40.0, ((0, 32),), jnp.float32),
        "bias_first": noise(seeds[14], (NB,), (0.077 * (LAT * LEN) ** 0.5), 64.0, ((0, 32),), jnp.float32),
        "qkv_second": jnp.clip(jnp.exp(math.log(16.384) - 1.3862944 * jax.random.uniform(seeds[15], (3 * D * D,), jnp.float32) ** shard_levels(seeds[15], (3 * D * D,), ((0, 32),), -0.2, 0.2)), 4.096, 16.384),
        "proj_second": jnp.clip(jnp.exp(math.log(0.65536) - 1.3862944 * jax.random.uniform(seeds[16], (D * D,), jnp.float32) ** shard_levels(seeds[16], (D * D,), ((0, 32),), -0.2, 0.2)), 0.16384, 0.65536),
        "fc1_second": jnp.clip(jnp.exp(math.log(16.384) - 1.3862944 * jax.random.uniform(seeds[17], (D * MLP,), jnp.float32) ** shard_levels(seeds[17], (D * MLP,), ((0, 32),), -0.2, 0.2)), 4.096, 16.384),
        "fc2_second": jnp.clip(jnp.exp(math.log(16.384) - 1.3862944 * jax.random.uniform(seeds[18], (MLP * D,), jnp.float32) ** shard_levels(seeds[18], (MLP * D,), ((0, 32),), -0.2, 0.2)), 4.096, 16.384),
        "ada_second": jnp.clip(jnp.exp(math.log(16.384) - 1.3862944 * jax.random.uniform(seeds[19], (SIXD, D), jnp.float32) ** shard_levels(seeds[19], (SIXD, D), ((0, 32),), -0.2, 0.2)), 4.096, 16.384),
        "bias_second": jnp.clip(jnp.exp(math.log(32.11264) - 1.3862944 * jax.random.uniform(seeds[20], (NB,), jnp.float32) ** shard_levels(seeds[20], (NB,), ((0, 32),), -0.2, 0.2)), 8.02816, 32.11264),
    }


NORM_EPS = 1e-06
ADAM_EPS = 1e-08
BETA_ONE = 0.9
BETA_TWO = 0.999
DECAY_RATE = 0.1
GELU_COEF = 0.7978845608028654

@jax.custom_vjp
def low(v):
    return lax.optimization_barrier(v.astype(jnp.bfloat16)).astype(jnp.float32)

@jax.custom_vjp
def low_back(v):
    return v

def low_keep(v):
    return (low(v), None)

def low_pass(kept, grad):
    return (grad,)

def back_keep(v):
    return (v, None)

def back_low(kept, grad):
    return (low(grad),)
low.defvjp(low_keep, low_pass)
low_back.defvjp(back_keep, back_low)

def silu_apply(values):
    return values * jax.nn.sigmoid(values)

def gelu_apply(values):
    return 0.5 * values * (1.0 + jnp.tanh(GELU_COEF * (values + 0.044715 * values * values * values)))

def layer_norm(values):
    average = lax.optimization_barrier(jnp.mean(values, axis=-1, keepdims=True))
    centered = values - average
    variance = lax.optimization_barrier(jnp.mean(centered * centered, axis=-1, keepdims=True))
    return centered * lax.rsqrt(variance + NORM_EPS)

def softmax_rows(scores):
    highest = lax.optimization_barrier(jnp.max(scores, axis=-1, keepdims=True))
    expo = jnp.exp(scores - highest)
    return expo / lax.optimization_barrier(jnp.sum(expo, axis=-1, keepdims=True))

def latent_block(pair, matrices, vectors):
    x_lat, mod_lat = pair
    w_qkv, w_proj, w_fc1, w_fc2 = matrices
    bias_qkv, bias_proj, bias_fc1, bias_fc2 = vectors
    shift_attn = mod_lat[0:D]
    scale_attn = mod_lat[D:2 * D]
    gate_attn = mod_lat[2 * D:3 * D]
    shift_mlp = mod_lat[3 * D:4 * D]
    scale_mlp = mod_lat[4 * D:5 * D]
    gate_mlp = mod_lat[5 * D:6 * D]
    hidden_a = low(layer_norm(x_lat) * (1.0 + scale_attn) + shift_attn)
    qkv = low_back(low(jnp.dot(hidden_a, w_qkv, precision=lax.Precision.HIGHEST) + bias_qkv))
    queries = qkv[:, :D].reshape(LEN, HEADS, HD)
    keys_all = qkv[:, D:2 * D].reshape(LEN, HEADS, HD)
    values_all = qkv[:, 2 * D:].reshape(LEN, HEADS, HD)
    scores = low_back(jnp.einsum('qhd,khd->hqk', queries, keys_all, precision=lax.Precision.HIGHEST) * HD ** (-0.5))
    probs = low(softmax_rows(scores))
    attended = jnp.einsum('hqk,khd->qhd', probs, values_all, precision=lax.Precision.HIGHEST).reshape(LEN, D)
    attended = low_back(low(attended))
    branch_a = low_back(jnp.dot(attended, w_proj, precision=lax.Precision.HIGHEST) + bias_proj)
    middle = x_lat + gate_attn * branch_a
    hidden_m = low(layer_norm(middle) * (1.0 + scale_mlp) + shift_mlp)
    pre_act = low_back(jnp.dot(hidden_m, w_fc1, precision=lax.Precision.HIGHEST) + bias_fc1)
    act = low(gelu_apply(pre_act))
    branch_m = low_back(jnp.dot(act, w_fc2, precision=lax.Precision.HIGHEST) + bias_fc2)
    return middle + gate_mlp * branch_m

def forward(inputs, conditions, qkv_weight, proj_weight, fc1_weight, fc2_weight, ada_weight, biases):
    silu_cond = low(silu_apply(conditions))
    modulation = jnp.dot(silu_cond, low(ada_weight).T, precision=lax.Precision.HIGHEST) + biases[4 * D + MLP:]
    matrices = (low(qkv_weight).reshape(D, 3 * D), low(proj_weight).reshape(D, D), low(fc1_weight).reshape(D, MLP), low(fc2_weight).reshape(MLP, D))
    bias_qkv = jnp.concatenate([biases[:D], jnp.zeros((D,), jnp.float32), biases[D:2 * D]])
    vectors = (bias_qkv, biases[2 * D:3 * D], biases[3 * D:3 * D + MLP], biases[3 * D + MLP:4 * D + MLP])
    block = jax.checkpoint(partial(latent_block, matrices=matrices, vectors=vectors))
    return lax.map(block, (inputs, modulation))

def adamw_update(weight, moment, second, gradient, step_rate):
    moment_new = BETA_ONE * moment + (1.0 - BETA_ONE) * gradient
    second_new = BETA_TWO * second + (1.0 - BETA_TWO) * gradient * gradient
    first_hat = moment_new / (1.0 - BETA_ONE ** STEP)
    second_hat = second_new / (1.0 - BETA_TWO ** STEP)
    weight_new = weight - step_rate * (first_hat / (jnp.sqrt(second_hat) + ADAM_EPS) + DECAY_RATE * weight)
    return (weight_new, moment_new, second_new)

def reference(latents, conditions, cotangent, qkv_weight, proj_weight, fc1_weight, fc2_weight, ada_weight, biases, qkv_first, proj_first, fc1_first, fc2_first, ada_first, bias_first, qkv_second, proj_second, fc1_second, fc2_second, ada_second, bias_second):
    inputs = latents.astype(jnp.float32)
    grad_out = cotangent.astype(jnp.float32)
    output, pull = jax.vjp(forward, inputs, conditions, qkv_weight, proj_weight, fc1_weight, fc2_weight, ada_weight, biases)
    gradients = pull(grad_out)
    rate_wide = 2.0 * D ** (-0.5)
    rate_proj = 2.0 * max(1, D * 256 // TOK_MIN) ** (-0.5)
    rate_fc2 = 2.0 * MLP ** (-0.5)
    new_qkv, qkv_m, qkv_s = adamw_update(qkv_weight, qkv_first, qkv_second, gradients[2], rate_wide)
    new_proj, proj_m, proj_s = adamw_update(proj_weight, proj_first, proj_second, gradients[3], rate_proj)
    new_fc1, fc1_m, fc1_s = adamw_update(fc1_weight, fc1_first, fc1_second, gradients[4], rate_wide)
    new_fc2, fc2_m, fc2_s = adamw_update(fc2_weight, fc2_first, fc2_second, gradients[5], rate_fc2)
    new_ada, ada_m, ada_s = adamw_update(ada_weight, ada_first, ada_second, gradients[6], rate_wide)
    new_bias, bias_m, bias_s = adamw_update(biases, bias_first, bias_second, gradients[7], 0.6)
    return (output.astype(jnp.bfloat16), gradients[0], gradients[1], new_qkv, new_proj, new_fc1, new_fc2, new_ada, new_bias, qkv_m, proj_m, fc1_m, fc2_m, ada_m, bias_m, qkv_s, proj_s, fc1_s, fc2_s, ada_s, bias_s)
```

```python
from functools import partial

import jax
import jax.numpy as jnp
from jax import lax
from jax.experimental import pallas as pl
from jax.experimental.pallas import tpu as pltpu
from jax.sharding import PartitionSpec as P

D = 1152
HEADS = 16
HD = 72
MLP = 4608
TOK_MIN = 1024
STEP = 10


NORM_EPS = 1e-06
ADAM_EPS = 1e-08
BETA_ONE = 0.9
BETA_TWO = 0.999
DECAY_RATE = 0.1
GELU_COEF = 0.7978845608028654


def silu_apply(values):
    return values * jax.nn.sigmoid(values)


def gelu_apply(values):
    return (
        0.5 * values * (1.0 + jnp.tanh(GELU_COEF * (values + 0.044715 * values * values * values)))
    )


def layer_norm(values):
    average = jnp.mean(values, axis=-1, keepdims=True)
    centered = values - average
    variance = jnp.mean(centered * centered, axis=-1, keepdims=True)
    inv_std = lax.rsqrt(variance + NORM_EPS)
    return (centered * inv_std, inv_std)


def norm_back(gradient, normed, inv_std):
    return inv_std * (
        gradient
        - jnp.mean(gradient, axis=-1, keepdims=True)
        - normed * jnp.mean(gradient * normed, axis=-1, keepdims=True)
    )


def adamw_update(weight, moment, second, gradient, step_rate):
    moment_new = BETA_ONE * moment + (1.0 - BETA_ONE) * gradient
    second_new = BETA_TWO * second + (1.0 - BETA_TWO) * gradient * gradient
    first_hat = moment_new / (1.0 - BETA_ONE**STEP)
    second_hat = second_new / (1.0 - BETA_TWO**STEP)
    weight_new = weight - step_rate * (
        first_hat / (jnp.sqrt(second_hat) + ADAM_EPS) + DECAY_RATE * weight
    )
    return (weight_new, moment_new, second_new)


def row_outer(left, right):
    return lax.dot_general(
        left, right, (((0,), (0,)), ((), ())), preferred_element_type=jnp.float32
    )


def times_transposed(left, right):
    return lax.dot_general(
        left, right, (((1,), (1,)), ((), ())), preferred_element_type=jnp.float32
    )


def gather_attention(qkv_weight, proj_weight):
    full_qkv, full_proj = (
        lax.all_gather(qkv_weight.astype(jnp.bfloat16), ("dp", "seq"), axis=0, tiled=True),
        lax.all_gather(proj_weight.astype(jnp.bfloat16), ("dp", "seq"), axis=0, tiled=True),
    )
    return (full_qkv.reshape(D, 3 * D), full_proj.reshape(D, D))


def gather_mlp(fc1_weight, fc2_weight):
    full_fc1, full_fc2 = (
        lax.all_gather(fc1_weight.astype(jnp.bfloat16), ("dp", "seq"), axis=0, tiled=True),
        lax.all_gather(fc2_weight.astype(jnp.bfloat16), ("dp", "seq"), axis=0, tiled=True),
    )
    return (full_fc1.reshape(D, MLP), full_fc2.reshape(MLP, D))


def to_groups(tensor):
    latent_count, length = (tensor.shape[0], tensor.shape[1])
    per_group = min(HEADS, 4)
    return jnp.moveaxis(
        tensor.reshape(latent_count, length, HEADS // per_group, per_group, HD), 2, 0
    )


def from_groups(tensor):
    shifted = jnp.moveaxis(tensor, 0, 2)
    return shifted.reshape(shifted.shape[0], shifted.shape[1], D)


def attend_group(operands):
    queries, keys_all, values_all = operands
    scores = jnp.einsum(
        "bqhd,bkhd->bhqk", queries, keys_all, preferred_element_type=jnp.float32
    ) * HD ** (-0.5)
    highest = jnp.max(scores, axis=-1, keepdims=True)
    expo = jnp.exp(scores - highest)
    totals = jnp.sum(expo, axis=-1, keepdims=True)
    probs_low = (expo / totals).astype(jnp.bfloat16)
    result = jnp.einsum(
        "bhqk,bkhd->bqhd", probs_low, values_all, preferred_element_type=jnp.float32
    )
    return (result, highest + jnp.log(totals))


def attend_back(operands):
    queries, keys_all, values_all, log_total, grad_att = operands
    scale = HD ** (-0.5)
    scores = (
        jnp.einsum("bqhd,bkhd->bhqk", queries, keys_all, preferred_element_type=jnp.float32) * scale
    )
    probs = jnp.exp(scores - log_total)
    probs_low = probs.astype(jnp.bfloat16)
    grad_probs = jnp.einsum(
        "bqhd,bkhd->bhqk", grad_att, values_all, preferred_element_type=jnp.float32
    )
    row_dot = jnp.sum(probs * grad_probs, axis=-1, keepdims=True)
    grad_scores = (probs * (grad_probs - row_dot)).astype(jnp.bfloat16)
    grad_queries = (
        jnp.einsum("bhqk,bkhd->bqhd", grad_scores, keys_all, preferred_element_type=jnp.float32)
        * scale
    )
    grad_keys = (
        jnp.einsum("bhqk,bqhd->bkhd", grad_scores, queries, preferred_element_type=jnp.float32)
        * scale
    )
    grad_values = jnp.einsum(
        "bhqk,bqhd->bkhd", probs_low, grad_att, preferred_element_type=jnp.float32
    )
    return (grad_queries, grad_keys, grad_values)


def per_device(
    latents,
    conditions,
    cotangent,
    qkv_weight,
    proj_weight,
    fc1_weight,
    fc2_weight,
    ada_weight,
    biases,
    qkv_first,
    proj_first,
    fc1_first,
    fc2_first,
    ada_first,
    bias_first,
    qkv_second,
    proj_second,
    fc1_second,
    fc2_second,
    ada_second,
    bias_second,
):
    latent_count, tokens = (latents.shape[0], latents.shape[1])
    silu_low = silu_apply(conditions).astype(jnp.bfloat16)
    all_silu = lax.all_gather(silu_low, "dp", axis=0, tiled=True)
    ada_low = ada_weight.astype(jnp.bfloat16)
    own_rows = times_transposed(all_silu, ada_low)
    mod_all, bias_all = (
        lax.all_gather(own_rows, ("dp", "seq"), axis=1, tiled=True),
        lax.all_gather(biases, ("dp", "seq"), axis=0, tiled=True),
    )
    first_latent = lax.axis_index("dp") * latent_count
    modulation = (
        lax.dynamic_slice_in_dim(mod_all, first_latent, latent_count, 0)
        + bias_all[4 * D + MLP :][None, :]
    )
    pieces = modulation.reshape(latent_count, 6, D)
    shift_attn = pieces[:, 0:1, :]
    scale_attn = pieces[:, 1:2, :]
    gate_attn = pieces[:, 2:3, :]
    shift_mlp = pieces[:, 3:4, :]
    scale_mlp = pieces[:, 4:5, :]
    gate_mlp = pieces[:, 5:6, :]
    w_qkv, w_proj = gather_attention(qkv_weight, proj_weight)
    w_fc1, w_fc2 = gather_mlp(fc1_weight, fc2_weight)
    inputs = latents.astype(jnp.float32)
    normed_a, inv_std_a = layer_norm(inputs)
    hidden_a = (normed_a * (1.0 + scale_attn) + shift_attn).astype(jnp.bfloat16).reshape(-1, D)
    bias_qkv = jnp.concatenate([bias_all[:D], jnp.zeros((D,), jnp.float32), bias_all[D : 2 * D]])
    qkv_low = (jnp.dot(hidden_a, w_qkv, preferred_element_type=jnp.float32) + bias_qkv).astype(
        jnp.bfloat16
    )
    qkv_low = qkv_low.reshape(latent_count, tokens, 3 * D)
    queries = qkv_low[..., :D]
    keys_own = qkv_low[..., D : 2 * D]
    values_own = qkv_low[..., 2 * D :]
    keys_all, values_all = (
        lax.all_gather(keys_own, "seq", axis=1, tiled=True),
        lax.all_gather(values_own, "seq", axis=1, tiled=True),
    )
    query_groups = to_groups(queries)
    key_groups = to_groups(keys_all)
    value_groups = to_groups(values_all)
    attended, log_total = lax.map(attend_group, (query_groups, key_groups, value_groups))
    attended_low = from_groups(attended).astype(jnp.bfloat16).reshape(-1, D)
    branch_a = (
        jnp.dot(attended_low, w_proj, preferred_element_type=jnp.float32) + bias_all[2 * D : 3 * D]
    ).reshape(latent_count, tokens, D)
    middle = inputs + gate_attn * branch_a
    normed_m, inv_std_m = layer_norm(middle)
    hidden_m = (normed_m * (1.0 + scale_mlp) + shift_mlp).astype(jnp.bfloat16).reshape(-1, D)
    pre_act = (
        jnp.dot(hidden_m, w_fc1, preferred_element_type=jnp.float32) + bias_all[3 * D : 3 * D + MLP]
    )
    act_low = gelu_apply(pre_act).astype(jnp.bfloat16)
    branch_m = (
        jnp.dot(act_low, w_fc2, preferred_element_type=jnp.float32)
        + bias_all[3 * D + MLP : 4 * D + MLP]
    ).reshape(latent_count, tokens, D)
    block_out = (middle + gate_mlp * branch_m).astype(jnp.bfloat16)
    grad_out = cotangent.astype(jnp.float32)
    grad_gate_m = jnp.sum(grad_out * branch_m, axis=1)
    grad_branch_m = (gate_mlp * grad_out).astype(jnp.bfloat16).reshape(-1, D)
    grad_fc2 = row_outer(act_low, grad_branch_m)
    grad_b2 = jnp.sum(grad_branch_m.astype(jnp.float32), axis=0)
    grad_act = times_transposed(grad_branch_m, w_fc2)
    gelu_pull = jax.vjp(gelu_apply, pre_act)[1]
    grad_pre = gelu_pull(grad_act)[0].astype(jnp.bfloat16)
    grad_fc1 = row_outer(hidden_m, grad_pre)
    grad_b1 = jnp.sum(grad_pre.astype(jnp.float32), axis=0)
    grad_hidden_m = times_transposed(grad_pre, w_fc1).reshape(latent_count, tokens, D)
    grad_scale_m = jnp.sum(grad_hidden_m * normed_m, axis=1)
    grad_shift_m = jnp.sum(grad_hidden_m, axis=1)
    grad_middle = grad_out + norm_back(grad_hidden_m * (1.0 + scale_mlp), normed_m, inv_std_m)
    grad_gate_a = jnp.sum(grad_middle * branch_a, axis=1)
    grad_branch_a = (gate_attn * grad_middle).astype(jnp.bfloat16).reshape(-1, D)
    grad_proj = row_outer(attended_low, grad_branch_a)
    grad_bproj = jnp.sum(grad_branch_a.astype(jnp.float32), axis=0)
    grad_att = (
        times_transposed(grad_branch_a, w_proj)
        .astype(jnp.bfloat16)
        .reshape(latent_count, tokens, D)
    )
    grad_queries, key_terms, value_terms = lax.map(
        attend_back, (query_groups, key_groups, value_groups, log_total, to_groups(grad_att))
    )
    grad_keys, grad_values = (
        lax.psum_scatter(
            from_groups(key_terms).astype(jnp.bfloat16), "seq", scatter_dimension=1, tiled=True
        ).astype(jnp.float32),
        lax.psum_scatter(
            from_groups(value_terms).astype(jnp.bfloat16), "seq", scatter_dimension=1, tiled=True
        ).astype(jnp.float32),
    )
    grad_qkv = jnp.concatenate([from_groups(grad_queries), grad_keys, grad_values], axis=-1)
    grad_qkv = grad_qkv.astype(jnp.bfloat16).reshape(-1, 3 * D)
    grad_wqkv = row_outer(hidden_a, grad_qkv)
    sums_qkv = jnp.sum(grad_qkv.astype(jnp.float32), axis=0)
    grad_hidden_a = times_transposed(grad_qkv, w_qkv).reshape(latent_count, tokens, D)
    grad_scale_a = jnp.sum(grad_hidden_a * normed_a, axis=1)
    grad_shift_a = jnp.sum(grad_hidden_a, axis=1)
    input_grad = grad_middle + norm_back(grad_hidden_a * (1.0 + scale_attn), normed_a, inv_std_a)
    summed_qkv, summed_proj, summed_fc1, summed_fc2 = (
        lax.psum_scatter(grad_wqkv.reshape(-1), ("dp", "seq"), scatter_dimension=0, tiled=True),
        lax.psum_scatter(grad_proj.reshape(-1), ("dp", "seq"), scatter_dimension=0, tiled=True),
        lax.psum_scatter(grad_fc1.reshape(-1), ("dp", "seq"), scatter_dimension=0, tiled=True),
        lax.psum_scatter(grad_fc2.reshape(-1), ("dp", "seq"), scatter_dimension=0, tiled=True),
    )
    grad_mod = jnp.concatenate(
        [grad_shift_a, grad_scale_a, grad_gate_a, grad_shift_m, grad_scale_m, grad_gate_m], axis=1
    )
    grad_bias = jnp.concatenate(
        [sums_qkv[:D], sums_qkv[2 * D :], grad_bproj, grad_b1, grad_b2, jnp.sum(grad_mod, axis=0)]
    )
    padded = lax.dynamic_update_slice_in_dim(
        jnp.zeros((mod_all.shape[0], 6 * D), jnp.float32), grad_mod, first_latent, 0
    )
    grad_rows, summed_bias = (
        lax.psum_scatter(padded, ("dp", "seq"), scatter_dimension=1, tiled=True),
        lax.psum_scatter(grad_bias, ("dp", "seq"), scatter_dimension=0, tiled=True),
    )
    summed_ada = jnp.dot(grad_rows.T, all_silu.astype(jnp.float32), precision=lax.Precision.HIGHEST)
    silu_terms = jnp.dot(grad_rows, ada_low.astype(jnp.float32), precision=lax.Precision.HIGHEST)
    grad_silu = lax.psum_scatter(
        silu_terms.astype(jnp.bfloat16), "dp", scatter_dimension=0, tiled=True
    ).astype(jnp.float32)
    grad_silu = lax.psum(grad_silu, "seq")
    silu_pull = jax.vjp(silu_apply, conditions)[1]
    cond_grad = silu_pull(grad_silu)[0]
    rate_wide = 2.0 * D ** (-0.5)
    rate_proj = 2.0 * max(1, D * 256 // TOK_MIN) ** (-0.5)
    rate_fc2 = 2.0 * MLP ** (-0.5)
    new_qkv, qkv_m, qkv_s = adamw_update(qkv_weight, qkv_first, qkv_second, summed_qkv, rate_wide)
    new_proj, proj_m, proj_s = adamw_update(
        proj_weight, proj_first, proj_second, summed_proj, rate_proj
    )
    new_fc1, fc1_m, fc1_s = adamw_update(fc1_weight, fc1_first, fc1_second, summed_fc1, rate_wide)
    new_fc2, fc2_m, fc2_s = adamw_update(fc2_weight, fc2_first, fc2_second, summed_fc2, rate_fc2)
    new_ada, ada_m, ada_s = adamw_update(ada_weight, ada_first, ada_second, summed_ada, rate_wide)
    new_bias, bias_m, bias_s = adamw_update(biases, bias_first, bias_second, summed_bias, 0.6)
    return (
        block_out,
        input_grad,
        cond_grad,
        new_qkv,
        new_proj,
        new_fc1,
        new_fc2,
        new_ada,
        new_bias,
        qkv_m,
        proj_m,
        fc1_m,
        fc2_m,
        ada_m,
        bias_m,
        qkv_s,
        proj_s,
        fc1_s,
        fc2_s,
        ada_s,
        bias_s,
    )


AXES = ("dp", "seq")
DEVICES = 32
ROWS = 144
UNIT = 36
SPLIT = 640
CORE_BIT = 1
X_BIT = 2
Y_BIT = 0


def flat_index():
    return lax.axis_index("dp") * 2 + lax.axis_index("seq")


def swap(value, bit):
    return lax.ppermute(value, AXES, [(i, i ^ (1 << bit)) for i in range(DEVICES)])


def along_z(value, step):
    pairs = [(i, i + 8 * step) for i in range(DEVICES) if 0 <= i + 8 * step < DEVICES]
    return lax.ppermute(value, AXES, pairs)


def relocate(value):
    pairs = [(i, (i & ~3) | ((i & 1) << 1) | ((i >> 1) & 1)) for i in range(DEVICES)]
    return lax.ppermute(value, AXES, pairs)


def take(value, index, axis):
    return lax.dynamic_index_in_dim(value, index, axis, keepdims=False)


def add_low(left, right):
    return (left.astype(jnp.float32) + right.astype(jnp.float32)).astype(jnp.bfloat16)


def gather_small(value, bits):
    me = flat_index()
    for bit in bits:
        other = swap(value, bit)
        upper = (me >> bit) & 1
        value = jnp.where(
            upper == 1,
            jnp.concatenate([other, value], axis=0),
            jnp.concatenate([value, other], axis=0),
        )
    return value


def gather_pieces(shard):
    z = flat_index() // 8
    lefts, rights = [], []
    rightward = leftward = shard
    for _ in range(3):
        rightward = along_z(rightward, 1)
        lefts.append(rightward)
        leftward = along_z(leftward, -1)
        rights.append(leftward)
    line = jnp.stack(lefts[::-1] + [shard] + rights)
    own = lax.dynamic_slice_in_dim(line, 3 - z, 4, 0)
    parts = []
    for low, high, order in ((0, SPLIT, (Y_BIT, X_BIT)), (SPLIT, D, (X_BIT, Y_BIT))):
        pieces = {0: own[:, :, low:high]}
        for bit in order + (CORE_BIT,):
            for p in sorted(pieces):
                pieces[p | (1 << bit)] = swap(pieces[p], bit)
        parts += [pieces[p] for p in range(8)]
    return parts


def unit_places(kind):
    if kind == "attention":
        return ((0, 0), (0, D), (0, 2 * D), (1, 0))
    return tuple((0, j * D) for j in range(4))


def block_shapes(kind):
    if kind == "attention":
        return ((8 * UNIT, 3 * D), (8 * UNIT, D))
    if kind == "fc1":
        return ((8 * UNIT, MLP),)
    return ((8 * ROWS, D),)


def assemble_kernel(me_ref, *refs, kind):
    outs, scratch = refs[16:-1], refs[-1]
    me = me_ref[0]
    for p in range(8):
        scratch[p ^ me, :, 0:SPLIT] = refs[p][0]
        scratch[p ^ me, :, SPLIT:D] = refs[8 + p][0]
    if kind == "fc2":
        for s in range(8):
            outs[0][ROWS * s : ROWS * (s + 1), :] = scratch[s]
    else:
        for j, (array, column) in enumerate(unit_places(kind)):
            outs[array][:, column : column + D] = jnp.concatenate(
                [scratch[s, UNIT * j : UNIT * (j + 1), :] for s in range(8)], axis=0
            )


def assemble(pieces, kind):
    blocks = block_shapes(kind)
    place = (flat_index() % 8).astype(jnp.int32).reshape(1)
    return pl.pallas_call(
        partial(assemble_kernel, kind=kind),
        out_shape=tuple(jax.ShapeDtypeStruct((4 * r, c), jnp.bfloat16) for r, c in blocks),
        grid_spec=pltpu.PrefetchScalarGridSpec(
            num_scalar_prefetch=1,
            grid=(4,),
            in_specs=[pl.BlockSpec((1, ROWS, SPLIT), lambda z, m: (z, 0, 0))] * 8
            + [pl.BlockSpec((1, ROWS, D - SPLIT), lambda z, m: (z, 0, 0))] * 8,
            out_specs=tuple(pl.BlockSpec(b, lambda z, m: (z, 0)) for b in blocks),
            scratch_shapes=[pltpu.VMEM((8, ROWS, D), jnp.bfloat16)],
        ),
        compiler_params=pltpu.CompilerParams(vmem_limit_bytes=40 * 2**20),
        cost_estimate=pl.CostEstimate(flops=0, bytes_accessed=21_000_000, transcendentals=0),
    )(place, *pieces)


def split_kernel(me_ref, *refs, kind):
    ins, keep_ref, send_ref, scratch = refs[:-3], refs[-3], refs[-2], refs[-1]
    core = (me_ref[0] // 2) % 2
    if kind == "fc2":
        for s in range(8):
            scratch[s] = ins[0][ROWS * s : ROWS * (s + 1), :]
    else:
        for j, (array, column) in enumerate(unit_places(kind)):
            for s in range(8):
                scratch[s, UNIT * j : UNIT * (j + 1), :] = ins[array][
                    UNIT * s : UNIT * (s + 1), column : column + D
                ]
    for x in range(2):
        for y in range(2):
            keep_ref[0, x, y] = scratch[4 * x + 2 * core + y]
            send_ref[0, x, y] = scratch[4 * x + 2 * (1 - core) + y]


def split_core(grads, kind):
    place = (flat_index() % 8).astype(jnp.int32).reshape(1)
    half = jax.ShapeDtypeStruct((4, 2, 2, ROWS, D), jnp.bfloat16)
    half_spec = pl.BlockSpec((1, 2, 2, ROWS, D), lambda z, m: (z, 0, 0, 0, 0))
    return pl.pallas_call(
        partial(split_kernel, kind=kind),
        out_shape=(half, half),
        grid_spec=pltpu.PrefetchScalarGridSpec(
            num_scalar_prefetch=1,
            grid=(4,),
            in_specs=[pl.BlockSpec(b, lambda z, m: (z, 0)) for b in block_shapes(kind)],
            out_specs=(half_spec, half_spec),
            scratch_shapes=[pltpu.VMEM((8, ROWS, D), jnp.bfloat16)],
        ),
        compiler_params=pltpu.CompilerParams(vmem_limit_bytes=40 * 2**20),
        cost_estimate=pl.CostEstimate(flops=0, bytes_accessed=21_000_000, transcendentals=0),
    )(place, *grads)


def scatter_sum(grads, kind):
    me = flat_index()
    y, x, z = me % 2, (me // 4) % 2, me // 8
    keep, send = split_core(grads, kind)
    half = add_low(keep, swap(send, CORE_BIT))
    parts = []
    for low, high, order in ((0, SPLIT, "xy"), (SPLIT, D, "yx")):
        part = half[..., low:high]
        for axis_name in order:
            if axis_name == "x":
                axis, index, bit = 1, x, X_BIT
            else:
                axis, index, bit = part.ndim - 3, y, Y_BIT
            part = add_low(take(part, index, axis), swap(take(part, 1 - index, axis), bit))
        parts.append(part)
    line = jnp.concatenate(parts, axis=-1)
    right = take(line, jnp.minimum(z + 3, 3), 0)
    left = take(line, jnp.maximum(z - 3, 0), 0)
    for step in (2, 1):
        right = add_low(take(line, jnp.minimum(z + step, 3), 0), along_z(right, 1))
        left = add_low(take(line, jnp.maximum(z - step, 0), 0), along_z(left, -1))
    total = take(line, z, 0).astype(jnp.float32)
    return total + along_z(right, 1).astype(jnp.float32) + along_z(left, -1).astype(jnp.float32)


def units_first(weight, units):
    rows = weight.reshape(UNIT, units, D)
    return jnp.swapaxes(rows, 0, 1).reshape(units * UNIT, D)


def units_last(shard, units):
    rows = shard.reshape(units, UNIT, D)
    return jnp.swapaxes(rows, 0, 1).reshape(-1)


def scatter_parts(payload):
    me = flat_index()
    buffer = payload.reshape((2,) * 5 + (payload.shape[-1],))
    for k, bit in enumerate((4, 3, 2, 1, 0)):
        upper = (me >> bit) & 1
        keep = take(buffer, upper, k)
        other = swap(take(buffer, 1 - upper, k), bit)
        buffer = jnp.where(
            upper == 1, jnp.stack([other, keep], axis=k), jnp.stack([keep, other], axis=k)
        )
    return buffer


def per_device_paired(
    latents,
    conditions,
    cotangent,
    qkv_weight,
    proj_weight,
    fc1_weight,
    fc2_weight,
    ada_weight,
    biases,
    qkv_first,
    proj_first,
    fc1_first,
    fc2_first,
    ada_first,
    bias_first,
    qkv_second,
    proj_second,
    fc1_second,
    fc2_second,
    ada_second,
    bias_second,
):
    tokens = latents.shape[1]
    me = flat_index()
    y, core = me % 2, (me // 2) % 2
    latent = (me // 4) * 2 + y

    shard_attention = jnp.concatenate(
        [
            units_first(qkv_weight.astype(jnp.bfloat16), 3),
            units_first(proj_weight.astype(jnp.bfloat16), 1),
        ],
        axis=0,
    )
    shard_fc1 = units_first(fc1_weight.astype(jnp.bfloat16), 4)
    shard_fc2 = fc2_weight.astype(jnp.bfloat16).reshape(ROWS, D)
    w_qkv, w_proj = assemble(gather_pieces(shard_attention), "attention")
    (w_fc1,) = assemble(gather_pieces(shard_fc1), "fc1")
    (w_fc2,) = assemble(gather_pieces(shard_fc2), "fc2")

    inputs = relocate(latents).reshape(tokens, D).astype(jnp.float32)
    grad_out = relocate(cotangent).reshape(tokens, D).astype(jnp.float32)

    silu_low = silu_apply(conditions).astype(jnp.bfloat16)
    all_silu = gather_small(silu_low.astype(jnp.float32), (1, 2, 3, 4)).astype(jnp.bfloat16)
    ada_low = ada_weight.astype(jnp.bfloat16)
    ada_rows = ada_low.shape[0]
    own_rows = times_transposed(all_silu, ada_low)
    small = jnp.concatenate([own_rows.reshape(-1), biases, jnp.zeros((136,), jnp.float32)])
    small_all = gather_small(small.reshape(1, 32, 128), (0, 1, 2, 3, 4)).reshape(DEVICES, 4096)
    mod_all = small_all[:, : 16 * ada_rows].reshape(DEVICES, 16, ada_rows)
    bias_all = small_all[:, 16 * ada_rows : 16 * ada_rows + biases.shape[0]].reshape(-1)
    modulation = take(mod_all, latent, 1).reshape(6, D) + bias_all[4 * D + MLP :].reshape(6, D)
    shift_attn, scale_attn, gate_attn, shift_mlp, scale_mlp, gate_mlp = (
        modulation[i : i + 1] for i in range(6)
    )

    normed_a, inv_std_a = layer_norm(inputs)
    hidden_a = (normed_a * (1.0 + scale_attn) + shift_attn).astype(jnp.bfloat16)
    bias_qkv = jnp.concatenate([bias_all[:D], jnp.zeros((D,), jnp.float32), bias_all[D : 2 * D]])
    qkv_low = (jnp.dot(hidden_a, w_qkv, preferred_element_type=jnp.float32) + bias_qkv).astype(
        jnp.bfloat16
    )
    keys_values = qkv_low[:, D:]
    other = swap(keys_values, CORE_BIT)
    keys_all = jnp.concatenate([keys_values[:, :D], other[:, :D]], axis=0)[None]
    values_all = jnp.concatenate([keys_values[:, D:], other[:, D:]], axis=0)[None]
    query_groups = to_groups(qkv_low[None, :, :D])
    key_groups = to_groups(keys_all)
    value_groups = to_groups(values_all)
    attended, log_total = lax.map(attend_group, (query_groups, key_groups, value_groups))
    attended_low = from_groups(attended).astype(jnp.bfloat16).reshape(-1, D)
    branch_a = (
        jnp.dot(attended_low, w_proj, preferred_element_type=jnp.float32) + bias_all[2 * D : 3 * D]
    )
    middle = inputs + gate_attn * branch_a
    normed_m, inv_std_m = layer_norm(middle)
    hidden_m = (normed_m * (1.0 + scale_mlp) + shift_mlp).astype(jnp.bfloat16)
    pre_act = (
        jnp.dot(hidden_m, w_fc1, preferred_element_type=jnp.float32) + bias_all[3 * D : 3 * D + MLP]
    )
    act_low = gelu_apply(pre_act).astype(jnp.bfloat16)
    grad_branch_m = (gate_mlp * grad_out).astype(jnp.bfloat16)
    grad_fc2 = row_outer(act_low, grad_branch_m).astype(jnp.bfloat16)
    summed_fc2 = scatter_sum((grad_fc2,), "fc2")
    branch_m = (
        jnp.dot(act_low, w_fc2, preferred_element_type=jnp.float32)
        + bias_all[3 * D + MLP : 4 * D + MLP]
    )
    block_out = relocate((middle + gate_mlp * branch_m).astype(jnp.bfloat16))[None]
    grad_gate_m = jnp.sum(grad_out * branch_m, axis=0)
    grad_b2 = jnp.sum(grad_branch_m.astype(jnp.float32), axis=0)
    grad_act = times_transposed(grad_branch_m, w_fc2)
    gelu_pull = jax.vjp(gelu_apply, pre_act)[1]
    grad_pre = gelu_pull(grad_act)[0].astype(jnp.bfloat16)
    grad_fc1 = row_outer(hidden_m, grad_pre).astype(jnp.bfloat16)
    summed_fc1 = scatter_sum((grad_fc1,), "fc1")
    grad_b1 = jnp.sum(grad_pre.astype(jnp.float32), axis=0)
    grad_hidden_m = times_transposed(grad_pre, w_fc1)
    grad_scale_m = jnp.sum(grad_hidden_m * normed_m, axis=0)
    grad_shift_m = jnp.sum(grad_hidden_m, axis=0)
    grad_middle = grad_out + norm_back(grad_hidden_m * (1.0 + scale_mlp), normed_m, inv_std_m)
    grad_gate_a = jnp.sum(grad_middle * branch_a, axis=0)
    grad_branch_a = (gate_attn * grad_middle).astype(jnp.bfloat16)
    grad_proj = row_outer(attended_low, grad_branch_a).astype(jnp.bfloat16)
    grad_bproj = jnp.sum(grad_branch_a.astype(jnp.float32), axis=0)
    grad_att = times_transposed(grad_branch_a, w_proj).astype(jnp.bfloat16)
    grad_queries, key_terms, value_terms = lax.map(
        attend_back, (query_groups, key_groups, value_groups, log_total, to_groups(grad_att[None]))
    )
    key_terms, value_terms = from_groups(key_terms)[0], from_groups(value_terms)[0]
    terms = jnp.concatenate([key_terms, value_terms], axis=-1)
    grad_keys_values = add_low(terms[:tokens], swap(terms[tokens:].astype(jnp.bfloat16), CORE_BIT))
    grad_qkv = jnp.concatenate(
        [from_groups(grad_queries)[0].astype(jnp.bfloat16), grad_keys_values], axis=-1
    )
    grad_wqkv = row_outer(hidden_a, grad_qkv).astype(jnp.bfloat16)
    summed_attention = scatter_sum((grad_wqkv, grad_proj), "attention")
    sums_qkv = jnp.sum(grad_qkv.astype(jnp.float32), axis=0)
    grad_hidden_a = times_transposed(grad_qkv, w_qkv)
    grad_scale_a = jnp.sum(grad_hidden_a * normed_a, axis=0)
    grad_shift_a = jnp.sum(grad_hidden_a, axis=0)
    input_grad = grad_middle + norm_back(grad_hidden_a * (1.0 + scale_attn), normed_a, inv_std_a)
    input_grad = jnp.where(
        y == core, input_grad, relocate(input_grad.astype(jnp.bfloat16)).astype(jnp.float32)
    )[None]

    grad_mod = jnp.concatenate(
        [grad_shift_a, grad_scale_a, grad_gate_a, grad_shift_m, grad_scale_m, grad_gate_m]
    )
    grad_bias = jnp.concatenate(
        [sums_qkv[:D], sums_qkv[2 * D :], grad_bproj, grad_b1, grad_b2, grad_mod]
    )
    payload = jnp.concatenate(
        [
            grad_mod.reshape(DEVICES, -1),
            grad_bias.reshape(DEVICES, -1),
            jnp.zeros((DEVICES, 48), jnp.float32),
        ],
        axis=1,
    )
    received = scatter_parts(payload)
    grad_rows = jnp.sum(received[..., :ada_rows], axis=3).reshape(16, ada_rows)
    summed_bias = jnp.sum(received.reshape(DEVICES, -1), axis=0)[
        ada_rows : ada_rows + biases.shape[0]
    ]
    summed_ada = jnp.dot(grad_rows.T, all_silu.astype(jnp.float32), precision=lax.Precision.HIGHEST)
    silu_terms = jnp.dot(grad_rows, ada_low.astype(jnp.float32), precision=lax.Precision.HIGHEST)
    grad_silu = silu_terms.reshape(2, 2, 2, 2, D)
    for bit in (4, 3, 2, 1):
        upper = (me >> bit) & 1
        grad_silu = take(grad_silu, upper, 0) + swap(take(grad_silu, 1 - upper, 0), bit)
    grad_silu = (grad_silu + swap(grad_silu, 0)).reshape(1, D)
    silu_pull = jax.vjp(silu_apply, conditions)[1]
    cond_grad = silu_pull(grad_silu)[0]

    rate_wide = 2.0 * D ** (-0.5)
    rate_proj = 2.0 * max(1, D * 256 // TOK_MIN) ** (-0.5)
    rate_fc2 = 2.0 * MLP ** (-0.5)
    summed_qkv = units_last(summed_attention[: 3 * UNIT], 3)
    summed_proj = summed_attention[3 * UNIT :].reshape(-1)
    new_qkv, qkv_m, qkv_s = adamw_update(qkv_weight, qkv_first, qkv_second, summed_qkv, rate_wide)
    new_proj, proj_m, proj_s = adamw_update(
        proj_weight, proj_first, proj_second, summed_proj, rate_proj
    )
    new_fc1, fc1_m, fc1_s = adamw_update(
        fc1_weight, fc1_first, fc1_second, units_last(summed_fc1, 4), rate_wide
    )
    new_fc2, fc2_m, fc2_s = adamw_update(
        fc2_weight, fc2_first, fc2_second, summed_fc2.reshape(-1), rate_fc2
    )
    new_ada, ada_m, ada_s = adamw_update(ada_weight, ada_first, ada_second, summed_ada, rate_wide)
    new_bias, bias_m, bias_s = adamw_update(biases, bias_first, bias_second, summed_bias, 0.6)
    return (
        block_out,
        input_grad,
        cond_grad,
        new_qkv,
        new_proj,
        new_fc1,
        new_fc2,
        new_ada,
        new_bias,
        qkv_m,
        proj_m,
        fc1_m,
        fc2_m,
        ada_m,
        bias_m,
        qkv_s,
        proj_s,
        fc1_s,
        fc2_s,
        ada_s,
        bias_s,
    )


def solution(mesh):
    in_specs = (
        P("dp", "seq", None),
        P("dp", None),
        P("dp", "seq", None),
        P(("dp", "seq")),
        P(("dp", "seq")),
        P(("dp", "seq")),
        P(("dp", "seq")),
        P(("dp", "seq"), None),
        P(("dp", "seq")),
        P(("dp", "seq")),
        P(("dp", "seq")),
        P(("dp", "seq")),
        P(("dp", "seq")),
        P(("dp", "seq"), None),
        P(("dp", "seq")),
        P(("dp", "seq")),
        P(("dp", "seq")),
        P(("dp", "seq")),
        P(("dp", "seq")),
        P(("dp", "seq"), None),
        P(("dp", "seq")),
    )
    out_specs = (
        P("dp", "seq", None),
        P("dp", "seq", None),
        P("dp", None),
        P(("dp", "seq")),
        P(("dp", "seq")),
        P(("dp", "seq")),
        P(("dp", "seq")),
        P(("dp", "seq"), None),
        P(("dp", "seq")),
        P(("dp", "seq")),
        P(("dp", "seq")),
        P(("dp", "seq")),
        P(("dp", "seq")),
        P(("dp", "seq"), None),
        P(("dp", "seq")),
        P(("dp", "seq")),
        P(("dp", "seq")),
        P(("dp", "seq")),
        P(("dp", "seq")),
        P(("dp", "seq"), None),
        P(("dp", "seq")),
    )
    eight = mesh.shape["dp"] == 16 and mesh.shape["seq"] == 2
    return jax.shard_map(
        per_device_paired if eight else per_device, mesh=mesh, in_specs=in_specs, out_specs=out_specs, check_vma=False
    )
```

```python
from functools import partial

import jax
import jax.numpy as jnp
from jax import lax
from jax.experimental import pallas as pl
from jax.experimental.pallas import tpu as pltpu
from jax.sharding import PartitionSpec as P

D = 1152
HEADS = 16
HD = 72
MLP = 4608
TOK_MIN = 1024
STEP = 10


NORM_EPS = 1e-06
ADAM_EPS = 1e-08
BETA_ONE = 0.9
BETA_TWO = 0.999
DECAY_RATE = 0.1
GELU_COEF = 0.7978845608028654


def silu_apply(values):
    return values * jax.nn.sigmoid(values)


def gelu_apply(values):
    return (
        0.5 * values * (1.0 + jnp.tanh(GELU_COEF * (values + 0.044715 * values * values * values)))
    )


def layer_norm(values):
    average = jnp.mean(values, axis=-1, keepdims=True)
    centered = values - average
    variance = jnp.mean(centered * centered, axis=-1, keepdims=True)
    inv_std = lax.rsqrt(variance + NORM_EPS)
    return (centered * inv_std, inv_std)


def norm_back(gradient, normed, inv_std):
    return inv_std * (
        gradient
        - jnp.mean(gradient, axis=-1, keepdims=True)
        - normed * jnp.mean(gradient * normed, axis=-1, keepdims=True)
    )


def adamw_update(weight, moment, second, gradient, step_rate):
    moment_new = BETA_ONE * moment + (1.0 - BETA_ONE) * gradient
    second_new = BETA_TWO * second + (1.0 - BETA_TWO) * gradient * gradient
    first_hat = moment_new / (1.0 - BETA_ONE**STEP)
    second_hat = second_new / (1.0 - BETA_TWO**STEP)
    weight_new = weight - step_rate * (
        first_hat / (jnp.sqrt(second_hat) + ADAM_EPS) + DECAY_RATE * weight
    )
    return (weight_new, moment_new, second_new)


def row_outer(left, right):
    return lax.dot_general(
        left, right, (((0,), (0,)), ((), ())), preferred_element_type=jnp.float32
    )


def times_transposed(left, right):
    return lax.dot_general(
        left, right, (((1,), (1,)), ((), ())), preferred_element_type=jnp.float32
    )


def gather_attention(qkv_weight, proj_weight):
    full_qkv, full_proj = (
        lax.all_gather(qkv_weight.astype(jnp.bfloat16), ("dp", "seq"), axis=0, tiled=True),
        lax.all_gather(proj_weight.astype(jnp.bfloat16), ("dp", "seq"), axis=0, tiled=True),
    )
    return (full_qkv.reshape(D, 3 * D), full_proj.reshape(D, D))


def gather_mlp(fc1_weight, fc2_weight):
    full_fc1, full_fc2 = (
        lax.all_gather(fc1_weight.astype(jnp.bfloat16), ("dp", "seq"), axis=0, tiled=True),
        lax.all_gather(fc2_weight.astype(jnp.bfloat16), ("dp", "seq"), axis=0, tiled=True),
    )
    return (full_fc1.reshape(D, MLP), full_fc2.reshape(MLP, D))


def to_groups(tensor):
    latent_count, length = (tensor.shape[0], tensor.shape[1])
    per_group = min(HEADS, 4)
    return jnp.moveaxis(
        tensor.reshape(latent_count, length, HEADS // per_group, per_group, HD), 2, 0
    )


def from_groups(tensor):
    shifted = jnp.moveaxis(tensor, 0, 2)
    return shifted.reshape(shifted.shape[0], shifted.shape[1], D)


def attend_group(operands):
    queries, keys_all, values_all = operands
    scores = jnp.einsum(
        "bqhd,bkhd->bhqk", queries, keys_all, preferred_element_type=jnp.float32
    ) * HD ** (-0.5)
    highest = jnp.max(scores, axis=-1, keepdims=True)
    expo = jnp.exp(scores - highest)
    totals = jnp.sum(expo, axis=-1, keepdims=True)
    probs_low = (expo / totals).astype(jnp.bfloat16)
    result = jnp.einsum(
        "bhqk,bkhd->bqhd", probs_low, values_all, preferred_element_type=jnp.float32
    )
    return (result, highest + jnp.log(totals))


def attend_back(operands):
    queries, keys_all, values_all, log_total, grad_att = operands
    scale = HD ** (-0.5)
    scores = (
        jnp.einsum("bqhd,bkhd->bhqk", queries, keys_all, preferred_element_type=jnp.float32) * scale
    )
    probs = jnp.exp(scores - log_total)
    probs_low = probs.astype(jnp.bfloat16)
    grad_probs = jnp.einsum(
        "bqhd,bkhd->bhqk", grad_att, values_all, preferred_element_type=jnp.float32
    )
    row_dot = jnp.sum(probs * grad_probs, axis=-1, keepdims=True)
    grad_scores = (probs * (grad_probs - row_dot)).astype(jnp.bfloat16)
    grad_queries = (
        jnp.einsum("bhqk,bkhd->bqhd", grad_scores, keys_all, preferred_element_type=jnp.float32)
        * scale
    )
    grad_keys = (
        jnp.einsum("bhqk,bqhd->bkhd", grad_scores, queries, preferred_element_type=jnp.float32)
        * scale
    )
    grad_values = jnp.einsum(
        "bhqk,bqhd->bkhd", probs_low, grad_att, preferred_element_type=jnp.float32
    )
    return (grad_queries, grad_keys, grad_values)


def per_device(
    latents,
    conditions,
    cotangent,
    qkv_weight,
    proj_weight,
    fc1_weight,
    fc2_weight,
    ada_weight,
    biases,
    qkv_first,
    proj_first,
    fc1_first,
    fc2_first,
    ada_first,
    bias_first,
    qkv_second,
    proj_second,
    fc1_second,
    fc2_second,
    ada_second,
    bias_second,
):
    latent_count, tokens = (latents.shape[0], latents.shape[1])
    silu_low = silu_apply(conditions).astype(jnp.bfloat16)
    all_silu = lax.all_gather(silu_low, "dp", axis=0, tiled=True)
    ada_low = ada_weight.astype(jnp.bfloat16)
    own_rows = times_transposed(all_silu, ada_low)
    mod_all, bias_all = (
        lax.all_gather(own_rows, ("dp", "seq"), axis=1, tiled=True),
        lax.all_gather(biases, ("dp", "seq"), axis=0, tiled=True),
    )
    first_latent = lax.axis_index("dp") * latent_count
    modulation = (
        lax.dynamic_slice_in_dim(mod_all, first_latent, latent_count, 0)
        + bias_all[4 * D + MLP :][None, :]
    )
    pieces = modulation.reshape(latent_count, 6, D)
    shift_attn = pieces[:, 0:1, :]
    scale_attn = pieces[:, 1:2, :]
    gate_attn = pieces[:, 2:3, :]
    shift_mlp = pieces[:, 3:4, :]
    scale_mlp = pieces[:, 4:5, :]
    gate_mlp = pieces[:, 5:6, :]
    w_qkv, w_proj = gather_attention(qkv_weight, proj_weight)
    w_fc1, w_fc2 = gather_mlp(fc1_weight, fc2_weight)
    inputs = latents.astype(jnp.float32)
    normed_a, inv_std_a = layer_norm(inputs)
    hidden_a = (normed_a * (1.0 + scale_attn) + shift_attn).astype(jnp.bfloat16).reshape(-1, D)
    bias_qkv = jnp.concatenate([bias_all[:D], jnp.zeros((D,), jnp.float32), bias_all[D : 2 * D]])
    qkv_low = (jnp.dot(hidden_a, w_qkv, preferred_element_type=jnp.float32) + bias_qkv).astype(
        jnp.bfloat16
    )
    qkv_low = qkv_low.reshape(latent_count, tokens, 3 * D)
    queries = qkv_low[..., :D]
    keys_own = qkv_low[..., D : 2 * D]
    values_own = qkv_low[..., 2 * D :]
    keys_all, values_all = (
        lax.all_gather(keys_own, "seq", axis=1, tiled=True),
        lax.all_gather(values_own, "seq", axis=1, tiled=True),
    )
    query_groups = to_groups(queries)
    key_groups = to_groups(keys_all)
    value_groups = to_groups(values_all)
    attended, log_total = lax.map(attend_group, (query_groups, key_groups, value_groups))
    attended_low = from_groups(attended).astype(jnp.bfloat16).reshape(-1, D)
    branch_a = (
        jnp.dot(attended_low, w_proj, preferred_element_type=jnp.float32) + bias_all[2 * D : 3 * D]
    ).reshape(latent_count, tokens, D)
    middle = inputs + gate_attn * branch_a
    normed_m, inv_std_m = layer_norm(middle)
    hidden_m = (normed_m * (1.0 + scale_mlp) + shift_mlp).astype(jnp.bfloat16).reshape(-1, D)
    pre_act = (
        jnp.dot(hidden_m, w_fc1, preferred_element_type=jnp.float32) + bias_all[3 * D : 3 * D + MLP]
    )
    act_low = gelu_apply(pre_act).astype(jnp.bfloat16)
    branch_m = (
        jnp.dot(act_low, w_fc2, preferred_element_type=jnp.float32)
        + bias_all[3 * D + MLP : 4 * D + MLP]
    ).reshape(latent_count, tokens, D)
    block_out = (middle + gate_mlp * branch_m).astype(jnp.bfloat16)
    grad_out = cotangent.astype(jnp.float32)
    grad_gate_m = jnp.sum(grad_out * branch_m, axis=1)
    grad_branch_m = (gate_mlp * grad_out).astype(jnp.bfloat16).reshape(-1, D)
    grad_fc2 = row_outer(act_low, grad_branch_m)
    grad_b2 = jnp.sum(grad_branch_m.astype(jnp.float32), axis=0)
    grad_act = times_transposed(grad_branch_m, w_fc2)
    gelu_pull = jax.vjp(gelu_apply, pre_act)[1]
    grad_pre = gelu_pull(grad_act)[0].astype(jnp.bfloat16)
    grad_fc1 = row_outer(hidden_m, grad_pre)
    grad_b1 = jnp.sum(grad_pre.astype(jnp.float32), axis=0)
    grad_hidden_m = times_transposed(grad_pre, w_fc1).reshape(latent_count, tokens, D)
    grad_scale_m = jnp.sum(grad_hidden_m * normed_m, axis=1)
    grad_shift_m = jnp.sum(grad_hidden_m, axis=1)
    grad_middle = grad_out + norm_back(grad_hidden_m * (1.0 + scale_mlp), normed_m, inv_std_m)
    grad_gate_a = jnp.sum(grad_middle * branch_a, axis=1)
    grad_branch_a = (gate_attn * grad_middle).astype(jnp.bfloat16).reshape(-1, D)
    grad_proj = row_outer(attended_low, grad_branch_a)
    grad_bproj = jnp.sum(grad_branch_a.astype(jnp.float32), axis=0)
    grad_att = (
        times_transposed(grad_branch_a, w_proj)
        .astype(jnp.bfloat16)
        .reshape(latent_count, tokens, D)
    )
    grad_queries, key_terms, value_terms = lax.map(
        attend_back, (query_groups, key_groups, value_groups, log_total, to_groups(grad_att))
    )
    grad_keys, grad_values = (
        lax.psum_scatter(
            from_groups(key_terms).astype(jnp.bfloat16), "seq", scatter_dimension=1, tiled=True
        ).astype(jnp.float32),
        lax.psum_scatter(
            from_groups(value_terms).astype(jnp.bfloat16), "seq", scatter_dimension=1, tiled=True
        ).astype(jnp.float32),
    )
    grad_qkv = jnp.concatenate([from_groups(grad_queries), grad_keys, grad_values], axis=-1)
    grad_qkv = grad_qkv.astype(jnp.bfloat16).reshape(-1, 3 * D)
    grad_wqkv = row_outer(hidden_a, grad_qkv)
    sums_qkv = jnp.sum(grad_qkv.astype(jnp.float32), axis=0)
    grad_hidden_a = times_transposed(grad_qkv, w_qkv).reshape(latent_count, tokens, D)
    grad_scale_a = jnp.sum(grad_hidden_a * normed_a, axis=1)
    grad_shift_a = jnp.sum(grad_hidden_a, axis=1)
    input_grad = grad_middle + norm_back(grad_hidden_a * (1.0 + scale_attn), normed_a, inv_std_a)
    summed_qkv, summed_proj, summed_fc1, summed_fc2 = (
        lax.psum_scatter(grad_wqkv.reshape(-1), ("dp", "seq"), scatter_dimension=0, tiled=True),
        lax.psum_scatter(grad_proj.reshape(-1), ("dp", "seq"), scatter_dimension=0, tiled=True),
        lax.psum_scatter(grad_fc1.reshape(-1), ("dp", "seq"), scatter_dimension=0, tiled=True),
        lax.psum_scatter(grad_fc2.reshape(-1), ("dp", "seq"), scatter_dimension=0, tiled=True),
    )
    grad_mod = jnp.concatenate(
        [grad_shift_a, grad_scale_a, grad_gate_a, grad_shift_m, grad_scale_m, grad_gate_m], axis=1
    )
    grad_bias = jnp.concatenate(
        [sums_qkv[:D], sums_qkv[2 * D :], grad_bproj, grad_b1, grad_b2, jnp.sum(grad_mod, axis=0)]
    )
    padded = lax.dynamic_update_slice_in_dim(
        jnp.zeros((mod_all.shape[0], 6 * D), jnp.float32), grad_mod, first_latent, 0
    )
    grad_rows, summed_bias = (
        lax.psum_scatter(padded, ("dp", "seq"), scatter_dimension=1, tiled=True),
        lax.psum_scatter(grad_bias, ("dp", "seq"), scatter_dimension=0, tiled=True),
    )
    summed_ada = jnp.dot(grad_rows.T, all_silu.astype(jnp.float32), precision=lax.Precision.HIGHEST)
    silu_terms = jnp.dot(grad_rows, ada_low.astype(jnp.float32), precision=lax.Precision.HIGHEST)
    grad_silu = lax.psum_scatter(
        silu_terms.astype(jnp.bfloat16), "dp", scatter_dimension=0, tiled=True
    ).astype(jnp.float32)
    grad_silu = lax.psum(grad_silu, "seq")
    silu_pull = jax.vjp(silu_apply, conditions)[1]
    cond_grad = silu_pull(grad_silu)[0]
    rate_wide = 2.0 * D ** (-0.5)
    rate_proj = 2.0 * max(1, D * 256 // TOK_MIN) ** (-0.5)
    rate_fc2 = 2.0 * MLP ** (-0.5)
    new_qkv, qkv_m, qkv_s = adamw_update(qkv_weight, qkv_first, qkv_second, summed_qkv, rate_wide)
    new_proj, proj_m, proj_s = adamw_update(
        proj_weight, proj_first, proj_second, summed_proj, rate_proj
    )
    new_fc1, fc1_m, fc1_s = adamw_update(fc1_weight, fc1_first, fc1_second, summed_fc1, rate_wide)
    new_fc2, fc2_m, fc2_s = adamw_update(fc2_weight, fc2_first, fc2_second, summed_fc2, rate_fc2)
    new_ada, ada_m, ada_s = adamw_update(ada_weight, ada_first, ada_second, summed_ada, rate_wide)
    new_bias, bias_m, bias_s = adamw_update(biases, bias_first, bias_second, summed_bias, 0.6)
    return (
        block_out,
        input_grad,
        cond_grad,
        new_qkv,
        new_proj,
        new_fc1,
        new_fc2,
        new_ada,
        new_bias,
        qkv_m,
        proj_m,
        fc1_m,
        fc2_m,
        ada_m,
        bias_m,
        qkv_s,
        proj_s,
        fc1_s,
        fc2_s,
        ada_s,
        bias_s,
    )


AXES = ("dp", "seq")
DEVICES = 32
ROWS = 144
UNIT = 36
SPLIT = 640
CORE_BIT = 1
X_BIT = 2
Y_BIT = 0


def flat_index():
    return lax.axis_index("dp") * 2 + lax.axis_index("seq")


def swap(value, bit):
    return lax.ppermute(value, AXES, [(i, i ^ (1 << bit)) for i in range(DEVICES)])


def same_column():
    return [[z * 4 + r for z in range(4)] for r in range(4)]


def after(value, *others):
    return lax.optimization_barrier((value,) + others)[0]


def relocate(value):
    pairs = [(i, i ^ 3) for i in range(DEVICES) if (i ^ (i >> 1)) & 1]
    me = flat_index()
    return jnp.where(((me ^ (me >> 1)) & 1) == 1, lax.ppermute(value, AXES, pairs), value)


def take(value, index, axis):
    return lax.dynamic_index_in_dim(value, index, axis, keepdims=False)


def add_low(left, right):
    return (left.astype(jnp.float32) + right.astype(jnp.float32)).astype(jnp.bfloat16)


def exchange(payload):
    return lax.all_to_all(payload, AXES, 0, 0, tiled=True)


def gather_line(shard):
    return lax.all_gather(shard, "dp", axis=0, axis_index_groups=same_column())


def column_parts(own):
    return (own[None, :, :, :SPLIT], own[None, :, :, SPLIT:])


def widen(parts, bits):
    return tuple(
        jnp.concatenate([part, swap(part, bit)], axis=0) for part, bit in zip(parts, bits)
    )


def gather_first(own):
    return widen(column_parts(own), (Y_BIT, X_BIT))


def gather_second(parts):
    return tuple(swap(part, bit) for part, bit in zip(parts, (X_BIT, Y_BIT)))


def gather_cores(parts, others):
    return tuple(
        (part, other, swap(part, CORE_BIT), swap(other, CORE_BIT))
        for part, other in zip(parts, others)
    )


def unit_places(kind):
    if kind == "attention":
        return ((0, 0), (0, D), (0, 2 * D), (1, 0))
    return tuple((0, j * D) for j in range(4))


def block_shapes(kind):
    if kind == "attention":
        return ((8 * UNIT, 3 * D), (8 * UNIT, D))
    if kind == "fc1":
        return ((8 * UNIT, MLP),)
    return ((8 * ROWS, D),)


PLACES = (((0, 1), (4, 5), (2, 3), (6, 7)), ((0, 4), (1, 5), (2, 6), (3, 7)))


def assemble_kernel(me_ref, *refs, kind):
    outs, scratch = refs[8:-1], refs[-1]
    me = me_ref[0]
    for part, (low, high) in enumerate(((0, SPLIT), (SPLIT, D))):
        for k in range(4):
            for i in range(2):
                scratch[PLACES[part][k][i] ^ me, :, low:high] = refs[part * 4 + k][i, 0]
    if kind == "fc2":
        for s in range(8):
            outs[0][ROWS * s : ROWS * (s + 1), :] = scratch[s]
    else:
        for j, (array, column) in enumerate(unit_places(kind)):
            outs[array][:, column : column + D] = jnp.concatenate(
                [scratch[s, UNIT * j : UNIT * (j + 1), :] for s in range(8)], axis=0
            )


def assemble(pieces, kind):
    blocks = block_shapes(kind)
    place = (flat_index() % 8).astype(jnp.int32).reshape(1)
    return pl.pallas_call(
        partial(assemble_kernel, kind=kind),
        out_shape=tuple(jax.ShapeDtypeStruct((4 * r, c), jnp.bfloat16) for r, c in blocks),
        grid_spec=pltpu.PrefetchScalarGridSpec(
            num_scalar_prefetch=1,
            grid=(4,),
            in_specs=[pl.BlockSpec((2, 1, ROWS, SPLIT), lambda z, m: (0, z, 0, 0))] * 4
            + [pl.BlockSpec((2, 1, ROWS, D - SPLIT), lambda z, m: (0, z, 0, 0))] * 4,
            out_specs=tuple(pl.BlockSpec(b, lambda z, m: (z, 0)) for b in blocks),
            scratch_shapes=[pltpu.VMEM((8, ROWS, D), jnp.bfloat16)],
        ),
        compiler_params=pltpu.CompilerParams(vmem_limit_bytes=40 * 2**20),
        cost_estimate=pl.CostEstimate(flops=0, bytes_accessed=21_000_000, transcendentals=0),
    )(place, *pieces[0], *pieces[1])


def split_kernel(me_ref, *refs, kind):
    ins, keep_ref, send_ref, scratch = refs[:-3], refs[-3], refs[-2], refs[-1]
    core = (me_ref[0] // 2) % 2
    if kind == "fc2":
        for s in range(8):
            scratch[s] = ins[0][ROWS * s : ROWS * (s + 1), :]
    else:
        for j, (array, column) in enumerate(unit_places(kind)):
            for s in range(8):
                scratch[s, UNIT * j : UNIT * (j + 1), :] = ins[array][
                    UNIT * s : UNIT * (s + 1), column : column + D
                ]
    for x in range(2):
        for y in range(2):
            keep_ref[0, x, y] = scratch[4 * x + 2 * core + y]
            send_ref[0, x, y] = scratch[4 * x + 2 * (1 - core) + y]


def split_core(grads, kind):
    place = (flat_index() % 8).astype(jnp.int32).reshape(1)
    half = jax.ShapeDtypeStruct((4, 2, 2, ROWS, D), jnp.bfloat16)
    half_spec = pl.BlockSpec((1, 2, 2, ROWS, D), lambda z, m: (z, 0, 0, 0, 0))
    return pl.pallas_call(
        partial(split_kernel, kind=kind),
        out_shape=(half, half),
        grid_spec=pltpu.PrefetchScalarGridSpec(
            num_scalar_prefetch=1,
            grid=(4,),
            in_specs=[pl.BlockSpec(b, lambda z, m: (z, 0)) for b in block_shapes(kind)],
            out_specs=(half_spec, half_spec),
            scratch_shapes=[pltpu.VMEM((8, ROWS, D), jnp.bfloat16)],
        ),
        compiler_params=pltpu.CompilerParams(vmem_limit_bytes=40 * 2**20),
        cost_estimate=pl.CostEstimate(flops=0, bytes_accessed=21_000_000, transcendentals=0),
    )(place, *grads)


def halve(parts, names):
    me = flat_index()
    out = []
    for part, name in zip(parts, names):
        axis, bit = (1, X_BIT) if name == "x" else (part.ndim - 3, Y_BIT)
        index = (me >> bit) & 1
        out.append(add_low(take(part, index, axis), swap(take(part, 1 - index, axis), bit)))
    return tuple(out)


def scatter_cores(keep, send):
    return add_low(keep, swap(send, CORE_BIT))


def scatter_first(half):
    return halve((half[..., :SPLIT], half[..., SPLIT:]), "xy")


def scatter_second(parts):
    return halve(parts, "yx")


def scatter_line(parts):
    return lax.psum_scatter(
        jnp.concatenate(parts, axis=-1),
        "dp",
        scatter_dimension=0,
        axis_index_groups=same_column(),
    ).astype(jnp.float32)


SCORE_SCALE = HD ** (-0.5) * 1.4426950408889634


def per_head(ref, row, width, target, first):
    for h in range(HEADS):
        lane = first + HD * h
        target[h, row : row + width, 0:HD] = ref[:, lane : lane + HD]


def side_by_side(source, row, width, ref, first):
    for h in range(HEADS):
        lane = first + HD * h
        ref[:, lane : lane + HD] = source[h, row : row + width, 0:HD]


def attend_kernel(own_ref, other_ref, out_ref, qs, ks, vs):
    tokens = own_ref.shape[0]
    per_head(own_ref, 0, tokens, qs, 0)
    per_head(own_ref, 0, tokens, ks, D)
    per_head(own_ref, 0, tokens, vs, 2 * D)
    per_head(other_ref, tokens, tokens, ks, 0)
    per_head(other_ref, tokens, tokens, vs, D)

    def one_head(h, carry):
        scores = times_transposed(qs[h, :, 0:HD], ks[h, :, 0:HD]) * SCORE_SCALE
        expo = jnp.exp2(scores - jnp.max(scores, axis=-1, keepdims=True))
        inverse = 1.0 / jnp.sum(expo, axis=-1, keepdims=True)
        probs_low = (expo * inverse).astype(jnp.bfloat16)
        result = jnp.dot(probs_low, vs[h, :, 0:HD], preferred_element_type=jnp.float32)
        qs[h, :, 0:HD] = result.astype(jnp.bfloat16)
        return carry

    lax.fori_loop(0, HEADS, one_head, 0, unroll=4)
    side_by_side(qs, 0, tokens, out_ref, 0)


def attend(own, other):
    tokens = own.shape[0]
    return pl.pallas_call(
        attend_kernel,
        out_shape=jax.ShapeDtypeStruct((tokens, D), jnp.bfloat16),
        scratch_shapes=[
            pltpu.VMEM((HEADS, tokens, 128), jnp.bfloat16),
            pltpu.VMEM((HEADS, 2 * tokens, 128), jnp.bfloat16),
            pltpu.VMEM((HEADS, 2 * tokens, 128), jnp.bfloat16),
        ],
        compiler_params=pltpu.CompilerParams(vmem_limit_bytes=48 * 2**20),
        cost_estimate=pl.CostEstimate(
            flops=8 * tokens * tokens * D, bytes_accessed=14 * tokens * D, transcendentals=0
        ),
    )(own, other)


def attend_back_kernel(
    own_ref, other_ref, grad_ref, dq_ref, near_ref, far_ref, qs, gs, ks, vs
):
    tokens = own_ref.shape[0]
    per_head(own_ref, 0, tokens, qs, 0)
    per_head(own_ref, 0, tokens, ks, D)
    per_head(own_ref, 0, tokens, vs, 2 * D)
    per_head(other_ref, tokens, tokens, ks, 0)
    per_head(other_ref, tokens, tokens, vs, D)
    per_head(grad_ref, 0, tokens, gs, 0)
    scale = HD ** (-0.5)

    def one_head(h, carry):
        keys, values = ks[h, :, 0:HD], vs[h, :, 0:HD]
        queries, grads = qs[h, :, 0:HD], gs[h, :, 0:HD]
        scores = times_transposed(keys, queries) * SCORE_SCALE
        expo = jnp.exp2(scores - jnp.max(scores, axis=0, keepdims=True))
        probs = expo * (1.0 / jnp.sum(expo, axis=0, keepdims=True))
        grad_values = jnp.dot(
            probs.astype(jnp.bfloat16), grads, preferred_element_type=jnp.float32
        )
        grad_probs = times_transposed(values, grads)
        row_dot = jnp.sum(probs * grad_probs, axis=0, keepdims=True)
        grad_scores = (probs * (grad_probs - row_dot)).astype(jnp.bfloat16)
        grad_keys = jnp.dot(grad_scores, queries, preferred_element_type=jnp.float32)
        grad_queries = row_outer(keys, grad_scores) * scale
        qs[h, :, 0:HD] = grad_queries.T.astype(jnp.bfloat16)
        ks[h, :, 0:HD] = (grad_keys * scale).astype(jnp.bfloat16)
        vs[h, :, 0:HD] = grad_values.astype(jnp.bfloat16)
        return carry

    lax.fori_loop(0, HEADS, one_head, 0, unroll=4)
    side_by_side(qs, 0, tokens, dq_ref, 0)
    side_by_side(ks, 0, tokens, near_ref, 0)
    side_by_side(vs, 0, tokens, near_ref, D)
    side_by_side(ks, tokens, tokens, far_ref, 0)
    side_by_side(vs, tokens, tokens, far_ref, D)


def attend_back_pair(own, other, grad):
    tokens = own.shape[0]
    return pl.pallas_call(
        attend_back_kernel,
        out_shape=(
            jax.ShapeDtypeStruct((tokens, D), jnp.bfloat16),
            jax.ShapeDtypeStruct((tokens, 2 * D), jnp.bfloat16),
            jax.ShapeDtypeStruct((tokens, 2 * D), jnp.bfloat16),
        ),
        scratch_shapes=[
            pltpu.VMEM((HEADS, tokens, 128), jnp.bfloat16),
            pltpu.VMEM((HEADS, tokens, 128), jnp.bfloat16),
            pltpu.VMEM((HEADS, 2 * tokens, 128), jnp.bfloat16),
            pltpu.VMEM((HEADS, 2 * tokens, 128), jnp.bfloat16),
        ],
        compiler_params=pltpu.CompilerParams(vmem_limit_bytes=56 * 2**20),
        cost_estimate=pl.CostEstimate(
            flops=20 * tokens * tokens * D, bytes_accessed=22 * tokens * D, transcendentals=0
        ),
    )(own, other, grad)


def units_first(weight, units):
    rows = weight.reshape(UNIT, units, D)
    return jnp.swapaxes(rows, 0, 1).reshape(units * UNIT, D)


def units_last(shard, units):
    rows = shard.reshape(units, UNIT, D)
    return jnp.swapaxes(rows, 0, 1).reshape(-1)


def per_device_paired(
    latents,
    conditions,
    cotangent,
    qkv_weight,
    proj_weight,
    fc1_weight,
    fc2_weight,
    ada_weight,
    biases,
    qkv_first,
    proj_first,
    fc1_first,
    fc2_first,
    ada_first,
    bias_first,
    qkv_second,
    proj_second,
    fc1_second,
    fc2_second,
    ada_second,
    bias_second,
):
    tokens = latents.shape[1]
    me = flat_index()
    y, core = me % 2, (me // 2) % 2
    latent = (me // 4) * 2 + y

    shard_attention = jnp.concatenate(
        [
            units_first(qkv_weight.astype(jnp.bfloat16), 3),
            units_first(proj_weight.astype(jnp.bfloat16), 1),
        ],
        axis=0,
    )
    shard_fc1 = units_first(fc1_weight.astype(jnp.bfloat16), 4)
    shard_fc2 = fc2_weight.astype(jnp.bfloat16).reshape(ROWS, D)
    line_attention = gather_line(shard_attention)
    line_fc1 = gather_line(after(shard_fc1, line_attention))
    line_fc2 = gather_line(after(shard_fc2, line_fc1))

    inputs = relocate(latents).reshape(tokens, D).astype(jnp.float32)
    grad_out = relocate(cotangent).reshape(tokens, D).astype(jnp.float32)

    silu_low = silu_apply(conditions).astype(jnp.bfloat16)
    all_silu = lax.all_to_all(
        jnp.broadcast_to(silu_low, (16, D)), "dp", 0, 0, tiled=True
    )
    ada_low = ada_weight.astype(jnp.bfloat16)
    ada_rows, bias_count = ada_low.shape[0], biases.shape[0]
    own_rows = times_transposed(all_silu, ada_low)
    by_device = jnp.broadcast_to(
        own_rows.reshape(8, 1, 2, ada_rows), (8, 2, 2, ada_rows)
    ).reshape(DEVICES, ada_rows)
    small = exchange(
        jnp.concatenate(
            [
                by_device,
                jnp.broadcast_to(biases[None], (DEVICES, bias_count)),
                jnp.zeros((DEVICES, 48), jnp.float32),
            ],
            axis=1,
        )
    )
    bias_all = small[:, ada_rows : ada_rows + bias_count].reshape(-1)
    modulation = small[:, :ada_rows].reshape(6, D) + bias_all[4 * D + MLP :].reshape(6, D)
    shift_attn, scale_attn, gate_attn, shift_mlp, scale_mlp, gate_mlp = (
        modulation[i : i + 1] for i in range(6)
    )

    first_attention = gather_first(after(line_attention, small))
    second_attention = gather_second(first_attention)
    w_qkv, w_proj = assemble(gather_cores(first_attention, second_attention), "attention")
    first_fc1 = gather_first(after(line_fc1, *second_attention))
    second_fc1 = gather_second(first_fc1)
    (w_fc1,) = assemble(gather_cores(first_fc1, second_fc1), "fc1")
    first_fc2 = gather_first(after(line_fc2, *first_fc1))
    second_fc2 = gather_second(first_fc2)
    (w_fc2,) = assemble(gather_cores(first_fc2, second_fc2), "fc2")

    normed_a, inv_std_a = layer_norm(inputs)
    hidden_a = (normed_a * (1.0 + scale_attn) + shift_attn).astype(jnp.bfloat16)
    bias_qkv = jnp.concatenate([bias_all[:D], jnp.zeros((D,), jnp.float32), bias_all[D : 2 * D]])
    qkv_low = (jnp.dot(after(hidden_a, *first_fc1), w_qkv, preferred_element_type=jnp.float32) + bias_qkv).astype(
        jnp.bfloat16
    )
    other = swap(qkv_low[:, D:], CORE_BIT)
    attended_low = attend(qkv_low, other)
    attended_low = after(attended_low, *second_fc1, *first_fc2)
    branch_a = (
        jnp.dot(attended_low, w_proj, preferred_element_type=jnp.float32) + bias_all[2 * D : 3 * D]
    )
    middle = inputs + gate_attn * branch_a
    normed_m, inv_std_m = layer_norm(middle)
    hidden_m = (normed_m * (1.0 + scale_mlp) + shift_mlp).astype(jnp.bfloat16)
    pre_act = (
        jnp.dot(hidden_m, w_fc1, preferred_element_type=jnp.float32) + bias_all[3 * D : 3 * D + MLP]
    )
    act_low = gelu_apply(pre_act).astype(jnp.bfloat16)
    grad_branch_m = (gate_mlp * grad_out).astype(jnp.bfloat16)
    act_low = after(act_low, *second_fc2)
    grad_fc2 = row_outer(act_low, grad_branch_m).astype(jnp.bfloat16)
    halves_fc2 = split_core((grad_fc2,), "fc2")
    half_fc2 = scatter_cores(*halves_fc2)
    branch_m = (
        jnp.dot(act_low, w_fc2, preferred_element_type=jnp.float32)
        + bias_all[3 * D + MLP : 4 * D + MLP]
    )
    block_out = relocate((middle + gate_mlp * branch_m).astype(jnp.bfloat16))[None]
    grad_gate_m = jnp.sum(grad_out * branch_m, axis=0)
    grad_b2 = jnp.sum(grad_branch_m.astype(jnp.float32), axis=0)
    grad_act = times_transposed(after(grad_branch_m, *halves_fc2), w_fc2)
    gelu_pull = jax.vjp(gelu_apply, pre_act)[1]
    grad_pre = gelu_pull(grad_act)[0].astype(jnp.bfloat16)
    grad_fc1 = row_outer(after(hidden_m, half_fc2), grad_pre).astype(jnp.bfloat16)
    first_grad_fc2 = scatter_first(half_fc2)
    halves_fc1 = split_core((grad_fc1,), "fc1")
    half_fc1 = scatter_cores(*halves_fc1)
    grad_b1 = jnp.sum(grad_pre.astype(jnp.float32), axis=0)
    grad_hidden_m = times_transposed(after(grad_pre, *halves_fc1), w_fc1)
    grad_scale_m = jnp.sum(grad_hidden_m * normed_m, axis=0)
    grad_shift_m = jnp.sum(grad_hidden_m, axis=0)
    grad_middle = grad_out + norm_back(grad_hidden_m * (1.0 + scale_mlp), normed_m, inv_std_m)
    grad_gate_a = jnp.sum(grad_middle * branch_a, axis=0)
    grad_branch_a = (gate_attn * grad_middle).astype(jnp.bfloat16)
    grad_proj = row_outer(attended_low, grad_branch_a).astype(jnp.bfloat16)
    grad_bproj = jnp.sum(grad_branch_a.astype(jnp.float32), axis=0)
    grad_att = times_transposed(grad_branch_a, w_proj).astype(jnp.bfloat16)
    grad_att = after(grad_att, half_fc1, *first_grad_fc2)
    second_grad_fc2 = scatter_second(first_grad_fc2)
    first_grad_fc1 = scatter_first(half_fc1)
    grad_queries, near, far = attend_back_pair(qkv_low, other, grad_att)
    grad_qkv = jnp.concatenate([grad_queries, add_low(near, swap(far, CORE_BIT))], axis=-1)
    late_hidden = after(hidden_a, *second_grad_fc2, *first_grad_fc1)
    summed_fc2 = scatter_line(second_grad_fc2)
    summed_fc1 = scatter_line(scatter_second(first_grad_fc1))
    grad_wqkv = row_outer(late_hidden, grad_qkv).astype(jnp.bfloat16)
    halves_attention = split_core((grad_wqkv, grad_proj), "attention")
    half_attention = scatter_cores(*halves_attention)
    first_grad_attention = scatter_first(half_attention)
    summed_attention = scatter_line(scatter_second(first_grad_attention))
    sums_qkv = jnp.sum(grad_qkv.astype(jnp.float32), axis=0)
    grad_hidden_a = times_transposed(after(grad_qkv, *halves_attention), w_qkv)
    grad_scale_a = jnp.sum(grad_hidden_a * normed_a, axis=0)
    grad_shift_a = jnp.sum(grad_hidden_a, axis=0)
    input_grad = grad_middle + norm_back(grad_hidden_a * (1.0 + scale_attn), normed_a, inv_std_a)
    moved_grad = relocate(after(input_grad.astype(jnp.bfloat16), half_attention))
    input_grad = jnp.where(y == core, input_grad, moved_grad.astype(jnp.float32))[None]

    grad_mod = jnp.concatenate(
        [grad_shift_a, grad_scale_a, grad_gate_a, grad_shift_m, grad_scale_m, grad_gate_m]
    )
    grad_bias = jnp.concatenate(
        [sums_qkv[:D], sums_qkv[2 * D :], grad_bproj, grad_b1, grad_b2, grad_mod]
    )
    payload = jnp.concatenate(
        [
            grad_mod.reshape(DEVICES, -1),
            grad_bias.reshape(DEVICES, -1),
            jnp.zeros((DEVICES, 48), jnp.float32),
        ],
        axis=1,
    )
    received = exchange(after(payload, half_attention))
    grad_rows = jnp.sum(received[:, :ada_rows].reshape(8, 2, 2, ada_rows), axis=1).reshape(
        16, ada_rows
    )
    summed_bias = jnp.sum(received[:, ada_rows : ada_rows + bias_count], axis=0)
    summed_ada = jnp.dot(grad_rows.T, all_silu.astype(jnp.float32), precision=lax.Precision.HIGHEST)
    silu_terms = jnp.dot(grad_rows, ada_low.astype(jnp.float32), precision=lax.Precision.HIGHEST)
    silu_terms = jnp.broadcast_to(silu_terms[:, None, :], (16, 2, D)).reshape(DEVICES, D)
    silu_terms = after(silu_terms, *first_grad_attention)
    grad_silu = jnp.sum(exchange(silu_terms), axis=0, keepdims=True)
    silu_pull = jax.vjp(silu_apply, conditions)[1]
    cond_grad = silu_pull(grad_silu)[0]

    rate_wide = 2.0 * D ** (-0.5)
    rate_proj = 2.0 * max(1, D * 256 // TOK_MIN) ** (-0.5)
    rate_fc2 = 2.0 * MLP ** (-0.5)
    summed_qkv = units_last(summed_attention[: 3 * UNIT], 3)
    summed_proj = summed_attention[3 * UNIT :].reshape(-1)
    new_qkv, qkv_m, qkv_s = adamw_update(qkv_weight, qkv_first, qkv_second, summed_qkv, rate_wide)
    new_proj, proj_m, proj_s = adamw_update(
        proj_weight, proj_first, proj_second, summed_proj, rate_proj
    )
    new_fc1, fc1_m, fc1_s = adamw_update(
        fc1_weight, fc1_first, fc1_second, units_last(summed_fc1, 4), rate_wide
    )
    new_fc2, fc2_m, fc2_s = adamw_update(
        fc2_weight, fc2_first, fc2_second, summed_fc2.reshape(-1), rate_fc2
    )
    new_ada, ada_m, ada_s = adamw_update(ada_weight, ada_first, ada_second, summed_ada, rate_wide)
    new_bias, bias_m, bias_s = adamw_update(biases, bias_first, bias_second, summed_bias, 0.6)
    return (
        block_out,
        input_grad,
        cond_grad,
        new_qkv,
        new_proj,
        new_fc1,
        new_fc2,
        new_ada,
        new_bias,
        qkv_m,
        proj_m,
        fc1_m,
        fc2_m,
        ada_m,
        bias_m,
        qkv_s,
        proj_s,
        fc1_s,
        fc2_s,
        ada_s,
        bias_s,
    )


def solution(mesh):
    in_specs = (
        P("dp", "seq", None),
        P("dp", None),
        P("dp", "seq", None),
        P(("dp", "seq")),
        P(("dp", "seq")),
        P(("dp", "seq")),
        P(("dp", "seq")),
        P(("dp", "seq"), None),
        P(("dp", "seq")),
        P(("dp", "seq")),
        P(("dp", "seq")),
        P(("dp", "seq")),
        P(("dp", "seq")),
        P(("dp", "seq"), None),
        P(("dp", "seq")),
        P(("dp", "seq")),
        P(("dp", "seq")),
        P(("dp", "seq")),
        P(("dp", "seq")),
        P(("dp", "seq"), None),
        P(("dp", "seq")),
    )
    out_specs = (
        P("dp", "seq", None),
        P("dp", "seq", None),
        P("dp", None),
        P(("dp", "seq")),
        P(("dp", "seq")),
        P(("dp", "seq")),
        P(("dp", "seq")),
        P(("dp", "seq"), None),
        P(("dp", "seq")),
        P(("dp", "seq")),
        P(("dp", "seq")),
        P(("dp", "seq")),
        P(("dp", "seq")),
        P(("dp", "seq"), None),
        P(("dp", "seq")),
        P(("dp", "seq")),
        P(("dp", "seq")),
        P(("dp", "seq")),
        P(("dp", "seq")),
        P(("dp", "seq"), None),
        P(("dp", "seq")),
    )
    eight = mesh.shape["dp"] == 16 and mesh.shape["seq"] == 2
    return jax.shard_map(
        per_device_paired if eight else per_device, mesh=mesh, in_specs=in_specs, out_specs=out_specs, check_vma=False
    )
```

```python
from functools import partial

import jax
import jax.numpy as jnp
from jax import lax
from jax.experimental import pallas as pl
from jax.experimental.pallas import tpu as pltpu
from jax.sharding import PartitionSpec as P

D = 1152
HEADS = 16
HD = 72
MLP = 4608
TOK_MIN = 1024
STEP = 10


NORM_EPS = 1e-06
ADAM_EPS = 1e-08
BETA_ONE = 0.9
BETA_TWO = 0.999
DECAY_RATE = 0.1
GELU_COEF = 0.7978845608028654


def silu_apply(values):
    return values * jax.nn.sigmoid(values)


def gelu_apply(values):
    return (
        0.5 * values * (1.0 + jnp.tanh(GELU_COEF * (values + 0.044715 * values * values * values)))
    )


def layer_norm(values):
    average = jnp.mean(values, axis=-1, keepdims=True)
    centered = values - average
    variance = jnp.mean(centered * centered, axis=-1, keepdims=True)
    inv_std = lax.rsqrt(variance + NORM_EPS)
    return (centered * inv_std, inv_std)


def norm_back(gradient, normed, inv_std):
    return inv_std * (
        gradient
        - jnp.mean(gradient, axis=-1, keepdims=True)
        - normed * jnp.mean(gradient * normed, axis=-1, keepdims=True)
    )


def adamw_update(weight, moment, second, gradient, step_rate):
    moment_new = BETA_ONE * moment + (1.0 - BETA_ONE) * gradient
    second_new = BETA_TWO * second + (1.0 - BETA_TWO) * gradient * gradient
    first_hat = moment_new / (1.0 - BETA_ONE**STEP)
    second_hat = second_new / (1.0 - BETA_TWO**STEP)
    weight_new = weight - step_rate * (
        first_hat / (jnp.sqrt(second_hat) + ADAM_EPS) + DECAY_RATE * weight
    )
    return (weight_new, moment_new, second_new)


def row_outer(left, right):
    return lax.dot_general(
        left, right, (((0,), (0,)), ((), ())), preferred_element_type=jnp.float32
    )


def times_transposed(left, right):
    return lax.dot_general(
        left, right, (((1,), (1,)), ((), ())), preferred_element_type=jnp.float32
    )


def gather_attention(qkv_weight, proj_weight):
    full_qkv, full_proj = (
        lax.all_gather(qkv_weight.astype(jnp.bfloat16), ("dp", "seq"), axis=0, tiled=True),
        lax.all_gather(proj_weight.astype(jnp.bfloat16), ("dp", "seq"), axis=0, tiled=True),
    )
    return (full_qkv.reshape(D, 3 * D), full_proj.reshape(D, D))


def gather_mlp(fc1_weight, fc2_weight):
    full_fc1, full_fc2 = (
        lax.all_gather(fc1_weight.astype(jnp.bfloat16), ("dp", "seq"), axis=0, tiled=True),
        lax.all_gather(fc2_weight.astype(jnp.bfloat16), ("dp", "seq"), axis=0, tiled=True),
    )
    return (full_fc1.reshape(D, MLP), full_fc2.reshape(MLP, D))


def to_groups(tensor):
    latent_count, length = (tensor.shape[0], tensor.shape[1])
    per_group = min(HEADS, 4)
    return jnp.moveaxis(
        tensor.reshape(latent_count, length, HEADS // per_group, per_group, HD), 2, 0
    )


def from_groups(tensor):
    shifted = jnp.moveaxis(tensor, 0, 2)
    return shifted.reshape(shifted.shape[0], shifted.shape[1], D)


def attend_group(operands):
    queries, keys_all, values_all = operands
    scores = jnp.einsum(
        "bqhd,bkhd->bhqk", queries, keys_all, preferred_element_type=jnp.float32
    ) * HD ** (-0.5)
    highest = jnp.max(scores, axis=-1, keepdims=True)
    expo = jnp.exp(scores - highest)
    totals = jnp.sum(expo, axis=-1, keepdims=True)
    probs_low = (expo / totals).astype(jnp.bfloat16)
    result = jnp.einsum(
        "bhqk,bkhd->bqhd", probs_low, values_all, preferred_element_type=jnp.float32
    )
    return (result, highest + jnp.log(totals))


def attend_back(operands):
    queries, keys_all, values_all, log_total, grad_att = operands
    scale = HD ** (-0.5)
    scores = (
        jnp.einsum("bqhd,bkhd->bhqk", queries, keys_all, preferred_element_type=jnp.float32) * scale
    )
    probs = jnp.exp(scores - log_total)
    probs_low = probs.astype(jnp.bfloat16)
    grad_probs = jnp.einsum(
        "bqhd,bkhd->bhqk", grad_att, values_all, preferred_element_type=jnp.float32
    )
    row_dot = jnp.sum(probs * grad_probs, axis=-1, keepdims=True)
    grad_scores = (probs * (grad_probs - row_dot)).astype(jnp.bfloat16)
    grad_queries = (
        jnp.einsum("bhqk,bkhd->bqhd", grad_scores, keys_all, preferred_element_type=jnp.float32)
        * scale
    )
    grad_keys = (
        jnp.einsum("bhqk,bqhd->bkhd", grad_scores, queries, preferred_element_type=jnp.float32)
        * scale
    )
    grad_values = jnp.einsum(
        "bhqk,bqhd->bkhd", probs_low, grad_att, preferred_element_type=jnp.float32
    )
    return (grad_queries, grad_keys, grad_values)


def per_device(
    latents,
    conditions,
    cotangent,
    qkv_weight,
    proj_weight,
    fc1_weight,
    fc2_weight,
    ada_weight,
    biases,
    qkv_first,
    proj_first,
    fc1_first,
    fc2_first,
    ada_first,
    bias_first,
    qkv_second,
    proj_second,
    fc1_second,
    fc2_second,
    ada_second,
    bias_second,
):
    latent_count, tokens = (latents.shape[0], latents.shape[1])
    silu_low = silu_apply(conditions).astype(jnp.bfloat16)
    all_silu = lax.all_gather(silu_low, "dp", axis=0, tiled=True)
    ada_low = ada_weight.astype(jnp.bfloat16)
    own_rows = times_transposed(all_silu, ada_low)
    mod_all, bias_all = (
        lax.all_gather(own_rows, ("dp", "seq"), axis=1, tiled=True),
        lax.all_gather(biases, ("dp", "seq"), axis=0, tiled=True),
    )
    first_latent = lax.axis_index("dp") * latent_count
    modulation = (
        lax.dynamic_slice_in_dim(mod_all, first_latent, latent_count, 0)
        + bias_all[4 * D + MLP :][None, :]
    )
    pieces = modulation.reshape(latent_count, 6, D)
    shift_attn = pieces[:, 0:1, :]
    scale_attn = pieces[:, 1:2, :]
    gate_attn = pieces[:, 2:3, :]
    shift_mlp = pieces[:, 3:4, :]
    scale_mlp = pieces[:, 4:5, :]
    gate_mlp = pieces[:, 5:6, :]
    w_qkv, w_proj = gather_attention(qkv_weight, proj_weight)
    w_fc1, w_fc2 = gather_mlp(fc1_weight, fc2_weight)
    inputs = latents.astype(jnp.float32)
    normed_a, inv_std_a = layer_norm(inputs)
    hidden_a = (normed_a * (1.0 + scale_attn) + shift_attn).astype(jnp.bfloat16).reshape(-1, D)
    bias_qkv = jnp.concatenate([bias_all[:D], jnp.zeros((D,), jnp.float32), bias_all[D : 2 * D]])
    qkv_low = (jnp.dot(hidden_a, w_qkv, preferred_element_type=jnp.float32) + bias_qkv).astype(
        jnp.bfloat16
    )
    qkv_low = qkv_low.reshape(latent_count, tokens, 3 * D)
    queries = qkv_low[..., :D]
    keys_own = qkv_low[..., D : 2 * D]
    values_own = qkv_low[..., 2 * D :]
    keys_all, values_all = (
        lax.all_gather(keys_own, "seq", axis=1, tiled=True),
        lax.all_gather(values_own, "seq", axis=1, tiled=True),
    )
    query_groups = to_groups(queries)
    key_groups = to_groups(keys_all)
    value_groups = to_groups(values_all)
    attended, log_total = lax.map(attend_group, (query_groups, key_groups, value_groups))
    attended_low = from_groups(attended).astype(jnp.bfloat16).reshape(-1, D)
    branch_a = (
        jnp.dot(attended_low, w_proj, preferred_element_type=jnp.float32) + bias_all[2 * D : 3 * D]
    ).reshape(latent_count, tokens, D)
    middle = inputs + gate_attn * branch_a
    normed_m, inv_std_m = layer_norm(middle)
    hidden_m = (normed_m * (1.0 + scale_mlp) + shift_mlp).astype(jnp.bfloat16).reshape(-1, D)
    pre_act = (
        jnp.dot(hidden_m, w_fc1, preferred_element_type=jnp.float32) + bias_all[3 * D : 3 * D + MLP]
    )
    act_low = gelu_apply(pre_act).astype(jnp.bfloat16)
    branch_m = (
        jnp.dot(act_low, w_fc2, preferred_element_type=jnp.float32)
        + bias_all[3 * D + MLP : 4 * D + MLP]
    ).reshape(latent_count, tokens, D)
    block_out = (middle + gate_mlp * branch_m).astype(jnp.bfloat16)
    grad_out = cotangent.astype(jnp.float32)
    grad_gate_m = jnp.sum(grad_out * branch_m, axis=1)
    grad_branch_m = (gate_mlp * grad_out).astype(jnp.bfloat16).reshape(-1, D)
    grad_fc2 = row_outer(act_low, grad_branch_m)
    grad_b2 = jnp.sum(grad_branch_m.astype(jnp.float32), axis=0)
    grad_act = times_transposed(grad_branch_m, w_fc2)
    gelu_pull = jax.vjp(gelu_apply, pre_act)[1]
    grad_pre = gelu_pull(grad_act)[0].astype(jnp.bfloat16)
    grad_fc1 = row_outer(hidden_m, grad_pre)
    grad_b1 = jnp.sum(grad_pre.astype(jnp.float32), axis=0)
    grad_hidden_m = times_transposed(grad_pre, w_fc1).reshape(latent_count, tokens, D)
    grad_scale_m = jnp.sum(grad_hidden_m * normed_m, axis=1)
    grad_shift_m = jnp.sum(grad_hidden_m, axis=1)
    grad_middle = grad_out + norm_back(grad_hidden_m * (1.0 + scale_mlp), normed_m, inv_std_m)
    grad_gate_a = jnp.sum(grad_middle * branch_a, axis=1)
    grad_branch_a = (gate_attn * grad_middle).astype(jnp.bfloat16).reshape(-1, D)
    grad_proj = row_outer(attended_low, grad_branch_a)
    grad_bproj = jnp.sum(grad_branch_a.astype(jnp.float32), axis=0)
    grad_att = (
        times_transposed(grad_branch_a, w_proj)
        .astype(jnp.bfloat16)
        .reshape(latent_count, tokens, D)
    )
    grad_queries, key_terms, value_terms = lax.map(
        attend_back, (query_groups, key_groups, value_groups, log_total, to_groups(grad_att))
    )
    grad_keys, grad_values = (
        lax.psum_scatter(
            from_groups(key_terms).astype(jnp.bfloat16), "seq", scatter_dimension=1, tiled=True
        ).astype(jnp.float32),
        lax.psum_scatter(
            from_groups(value_terms).astype(jnp.bfloat16), "seq", scatter_dimension=1, tiled=True
        ).astype(jnp.float32),
    )
    grad_qkv = jnp.concatenate([from_groups(grad_queries), grad_keys, grad_values], axis=-1)
    grad_qkv = grad_qkv.astype(jnp.bfloat16).reshape(-1, 3 * D)
    grad_wqkv = row_outer(hidden_a, grad_qkv)
    sums_qkv = jnp.sum(grad_qkv.astype(jnp.float32), axis=0)
    grad_hidden_a = times_transposed(grad_qkv, w_qkv).reshape(latent_count, tokens, D)
    grad_scale_a = jnp.sum(grad_hidden_a * normed_a, axis=1)
    grad_shift_a = jnp.sum(grad_hidden_a, axis=1)
    input_grad = grad_middle + norm_back(grad_hidden_a * (1.0 + scale_attn), normed_a, inv_std_a)
    summed_qkv, summed_proj, summed_fc1, summed_fc2 = (
        lax.psum_scatter(grad_wqkv.reshape(-1), ("dp", "seq"), scatter_dimension=0, tiled=True),
        lax.psum_scatter(grad_proj.reshape(-1), ("dp", "seq"), scatter_dimension=0, tiled=True),
        lax.psum_scatter(grad_fc1.reshape(-1), ("dp", "seq"), scatter_dimension=0, tiled=True),
        lax.psum_scatter(grad_fc2.reshape(-1), ("dp", "seq"), scatter_dimension=0, tiled=True),
    )
    grad_mod = jnp.concatenate(
        [grad_shift_a, grad_scale_a, grad_gate_a, grad_shift_m, grad_scale_m, grad_gate_m], axis=1
    )
    grad_bias = jnp.concatenate(
        [sums_qkv[:D], sums_qkv[2 * D :], grad_bproj, grad_b1, grad_b2, jnp.sum(grad_mod, axis=0)]
    )
    padded = lax.dynamic_update_slice_in_dim(
        jnp.zeros((mod_all.shape[0], 6 * D), jnp.float32), grad_mod, first_latent, 0
    )
    grad_rows, summed_bias = (
        lax.psum_scatter(padded, ("dp", "seq"), scatter_dimension=1, tiled=True),
        lax.psum_scatter(grad_bias, ("dp", "seq"), scatter_dimension=0, tiled=True),
    )
    summed_ada = jnp.dot(grad_rows.T, all_silu.astype(jnp.float32), precision=lax.Precision.HIGHEST)
    silu_terms = jnp.dot(grad_rows, ada_low.astype(jnp.float32), precision=lax.Precision.HIGHEST)
    grad_silu = lax.psum_scatter(
        silu_terms.astype(jnp.bfloat16), "dp", scatter_dimension=0, tiled=True
    ).astype(jnp.float32)
    grad_silu = lax.psum(grad_silu, "seq")
    silu_pull = jax.vjp(silu_apply, conditions)[1]
    cond_grad = silu_pull(grad_silu)[0]
    rate_wide = 2.0 * D ** (-0.5)
    rate_proj = 2.0 * max(1, D * 256 // TOK_MIN) ** (-0.5)
    rate_fc2 = 2.0 * MLP ** (-0.5)
    new_qkv, qkv_m, qkv_s = adamw_update(qkv_weight, qkv_first, qkv_second, summed_qkv, rate_wide)
    new_proj, proj_m, proj_s = adamw_update(
        proj_weight, proj_first, proj_second, summed_proj, rate_proj
    )
    new_fc1, fc1_m, fc1_s = adamw_update(fc1_weight, fc1_first, fc1_second, summed_fc1, rate_wide)
    new_fc2, fc2_m, fc2_s = adamw_update(fc2_weight, fc2_first, fc2_second, summed_fc2, rate_fc2)
    new_ada, ada_m, ada_s = adamw_update(ada_weight, ada_first, ada_second, summed_ada, rate_wide)
    new_bias, bias_m, bias_s = adamw_update(biases, bias_first, bias_second, summed_bias, 0.6)
    return (
        block_out,
        input_grad,
        cond_grad,
        new_qkv,
        new_proj,
        new_fc1,
        new_fc2,
        new_ada,
        new_bias,
        qkv_m,
        proj_m,
        fc1_m,
        fc2_m,
        ada_m,
        bias_m,
        qkv_s,
        proj_s,
        fc1_s,
        fc2_s,
        ada_s,
        bias_s,
    )


AXES = ("dp", "seq")
DEVICES = 32
ROWS = 144
UNIT = 36
SPLIT = 640
CORE_BIT = 1
X_BIT = 2
Y_BIT = 0


def flat_index():
    return lax.axis_index("dp") * 2 + lax.axis_index("seq")


def swap(value, bit):
    return lax.ppermute(value, AXES, [(i, i ^ (1 << bit)) for i in range(DEVICES)])


def same_column():
    return [[z * 4 + r for z in range(4)] for r in range(4)]


def after(value, *others):
    return lax.optimization_barrier((value,) + others)[0]


def all_after(values, *others):
    return lax.optimization_barrier(tuple(values) + others)[: len(values)]


def relocate(value):
    pairs = [(i, i ^ 3) for i in range(DEVICES) if (i ^ (i >> 1)) & 1]
    me = flat_index()
    return jnp.where(((me ^ (me >> 1)) & 1) == 1, lax.ppermute(value, AXES, pairs), value)


def take(value, index, axis):
    return lax.dynamic_index_in_dim(value, index, axis, keepdims=False)


def add_low(left, right):
    return (left.astype(jnp.float32) + right.astype(jnp.float32)).astype(jnp.bfloat16)


def exchange(payload):
    return lax.all_to_all(payload, AXES, 0, 0, tiled=True)


def gather_line(shard):
    return lax.all_gather(shard, "dp", axis=0, axis_index_groups=same_column())


def column_parts(own):
    return (own[None, ..., :SPLIT], own[None, ..., SPLIT:])


def swap_parts(parts, bits):
    return tuple(swap(part, bit) for part, bit in zip(parts, bits))


def widen(parts, others):
    return tuple(
        jnp.concatenate([part, other], axis=0) for part, other in zip(parts, others)
    )


FIRST_BITS = (Y_BIT, X_BIT)
SECOND_BITS = (X_BIT, Y_BIT)


def gather_cores(parts, others):
    return tuple(
        (part, other, swap(part, CORE_BIT), swap(other, CORE_BIT))
        for part, other in zip(parts, others)
    )


def unit_places(kind):
    if kind == "attention":
        return ((0, 0), (0, D), (0, 2 * D), (1, 0))
    return tuple((0, j * D) for j in range(4))


def block_shapes(kind):
    if kind == "attention":
        return ((8 * UNIT, 3 * D), (8 * UNIT, D))
    if kind == "fc1":
        return ((8 * UNIT, MLP),)
    return ((8 * ROWS, D),)


PLACES = (((0, 1), (4, 5), (2, 3), (6, 7)), ((0, 4), (1, 5), (2, 6), (3, 7)))


def assemble_kernel(me_ref, *refs, kind):
    outs, scratch = refs[8:-1], refs[-1]
    me = me_ref[0]
    for part, (low, high) in enumerate(((0, SPLIT), (SPLIT, D))):
        for k in range(4):
            for i in range(2):
                scratch[PLACES[part][k][i] ^ me, :, low:high] = refs[part * 4 + k][i, 0]
    if kind == "fc2":
        for s in range(8):
            outs[0][ROWS * s : ROWS * (s + 1), :] = scratch[s]
    else:
        for j, (array, column) in enumerate(unit_places(kind)):
            outs[array][:, column : column + D] = jnp.concatenate(
                [scratch[s, UNIT * j : UNIT * (j + 1), :] for s in range(8)], axis=0
            )


def assemble(pieces, kind):
    blocks = block_shapes(kind)
    place = (flat_index() % 8).astype(jnp.int32).reshape(1)
    return pl.pallas_call(
        partial(assemble_kernel, kind=kind),
        out_shape=tuple(jax.ShapeDtypeStruct((4 * r, c), jnp.bfloat16) for r, c in blocks),
        grid_spec=pltpu.PrefetchScalarGridSpec(
            num_scalar_prefetch=1,
            grid=(4,),
            in_specs=[pl.BlockSpec((2, 1, ROWS, SPLIT), lambda z, m: (0, z, 0, 0))] * 4
            + [pl.BlockSpec((2, 1, ROWS, D - SPLIT), lambda z, m: (0, z, 0, 0))] * 4,
            out_specs=tuple(pl.BlockSpec(b, lambda z, m: (z, 0)) for b in blocks),
            scratch_shapes=[pltpu.VMEM((8, ROWS, D), jnp.bfloat16)],
        ),
        compiler_params=pltpu.CompilerParams(vmem_limit_bytes=40 * 2**20),
        cost_estimate=pl.CostEstimate(flops=0, bytes_accessed=21_000_000, transcendentals=0),
    )(place, *pieces[0], *pieces[1])


def split_kernel(me_ref, *refs, kind):
    ins, keep_ref, send_ref, scratch = refs[:-3], refs[-3], refs[-2], refs[-1]
    core = (me_ref[0] // 2) % 2
    if kind == "fc2":
        for s in range(8):
            scratch[s] = ins[0][ROWS * s : ROWS * (s + 1), :]
    else:
        for j, (array, column) in enumerate(unit_places(kind)):
            for s in range(8):
                scratch[s, UNIT * j : UNIT * (j + 1), :] = ins[array][
                    UNIT * s : UNIT * (s + 1), column : column + D
                ]
    for x in range(2):
        for y in range(2):
            keep_ref[0, x, y] = scratch[4 * x + 2 * core + y]
            send_ref[0, x, y] = scratch[4 * x + 2 * (1 - core) + y]


def split_core(grads, kind):
    place = (flat_index() % 8).astype(jnp.int32).reshape(1)
    half = jax.ShapeDtypeStruct((4, 2, 2, ROWS, D), jnp.bfloat16)
    half_spec = pl.BlockSpec((1, 2, 2, ROWS, D), lambda z, m: (z, 0, 0, 0, 0))
    return pl.pallas_call(
        partial(split_kernel, kind=kind),
        out_shape=(half, half),
        grid_spec=pltpu.PrefetchScalarGridSpec(
            num_scalar_prefetch=1,
            grid=(4,),
            in_specs=[pl.BlockSpec(b, lambda z, m: (z, 0)) for b in block_shapes(kind)],
            out_specs=(half_spec, half_spec),
            scratch_shapes=[pltpu.VMEM((8, ROWS, D), jnp.bfloat16)],
        ),
        compiler_params=pltpu.CompilerParams(vmem_limit_bytes=40 * 2**20),
        cost_estimate=pl.CostEstimate(flops=0, bytes_accessed=21_000_000, transcendentals=0),
    )(place, *grads)


def halves(parts, names):
    me = flat_index()
    keeps, sends = [], []
    for part, name in zip(parts, names):
        axis, bit = (1, X_BIT) if name == "x" else (part.ndim - 3, Y_BIT)
        index = (me >> bit) & 1
        keeps.append(take(part, index, axis))
        sends.append(take(part, 1 - index, axis))
    return tuple(keeps), tuple(sends)


def add_parts(keeps, others):
    return tuple(add_low(keep, other) for keep, other in zip(keeps, others))


def scatter_cores(keep, send):
    return add_low(keep, swap(send, CORE_BIT))


def first_halves(half):
    return halves((half[..., :SPLIT], half[..., SPLIT:]), "xy")


def second_halves(parts):
    return halves(parts, "yx")


def scatter_line(parts):
    return lax.psum_scatter(
        jnp.concatenate(parts, axis=-1),
        "dp",
        scatter_dimension=0,
        axis_index_groups=same_column(),
    ).astype(jnp.float32)


SCORE_SCALE = HD ** (-0.5) * 1.4426950408889634


def per_head(ref, row, width, target, first):
    for h in range(HEADS):
        lane = first + HD * h
        target[h, row : row + width, 0:HD] = ref[:, lane : lane + HD]


def side_by_side(source, row, width, ref, first):
    for h in range(HEADS):
        lane = first + HD * h
        ref[:, lane : lane + HD] = source[h, row : row + width, 0:HD]


def attend_kernel(own_ref, other_ref, out_ref, qs, ks, vs):
    tokens = own_ref.shape[0]
    per_head(own_ref, 0, tokens, qs, 0)
    per_head(own_ref, 0, tokens, ks, D)
    per_head(own_ref, 0, tokens, vs, 2 * D)
    per_head(other_ref, tokens, tokens, ks, 0)
    per_head(other_ref, tokens, tokens, vs, D)

    def one_head(h, carry):
        scores = times_transposed(qs[h, :, 0:HD], ks[h, :, 0:HD]) * SCORE_SCALE
        expo = jnp.exp2(scores - jnp.max(scores, axis=-1, keepdims=True))
        inverse = 1.0 / jnp.sum(expo, axis=-1, keepdims=True)
        probs_low = (expo * inverse).astype(jnp.bfloat16)
        result = jnp.dot(probs_low, vs[h, :, 0:HD], preferred_element_type=jnp.float32)
        qs[h, :, 0:HD] = result.astype(jnp.bfloat16)
        return carry

    lax.fori_loop(0, HEADS, one_head, 0, unroll=4)
    side_by_side(qs, 0, tokens, out_ref, 0)


def attend(own, other):
    tokens = own.shape[0]
    return pl.pallas_call(
        attend_kernel,
        out_shape=jax.ShapeDtypeStruct((tokens, D), jnp.bfloat16),
        scratch_shapes=[
            pltpu.VMEM((HEADS, tokens, 128), jnp.bfloat16),
            pltpu.VMEM((HEADS, 2 * tokens, 128), jnp.bfloat16),
            pltpu.VMEM((HEADS, 2 * tokens, 128), jnp.bfloat16),
        ],
        compiler_params=pltpu.CompilerParams(vmem_limit_bytes=48 * 2**20),
        cost_estimate=pl.CostEstimate(
            flops=92 * tokens * tokens * D, bytes_accessed=14 * tokens * D, transcendentals=0
        ),
    )(own, other)


def attend_back_kernel(
    own_ref, other_ref, grad_ref, dq_ref, near_ref, far_ref, qs, gs, ks, vs
):
    tokens = own_ref.shape[0]
    per_head(own_ref, 0, tokens, qs, 0)
    per_head(own_ref, 0, tokens, ks, D)
    per_head(own_ref, 0, tokens, vs, 2 * D)
    per_head(other_ref, tokens, tokens, ks, 0)
    per_head(other_ref, tokens, tokens, vs, D)
    per_head(grad_ref, 0, tokens, gs, 0)
    scale = HD ** (-0.5)

    def one_head(h, carry):
        keys, values = ks[h, :, 0:HD], vs[h, :, 0:HD]
        queries, grads = qs[h, :, 0:HD], gs[h, :, 0:HD]
        scores = times_transposed(keys, queries) * SCORE_SCALE
        expo = jnp.exp2(scores - jnp.max(scores, axis=0, keepdims=True))
        probs = expo * (1.0 / jnp.sum(expo, axis=0, keepdims=True))
        grad_values = jnp.dot(
            probs.astype(jnp.bfloat16), grads, preferred_element_type=jnp.float32
        )
        grad_probs = times_transposed(values, grads)
        row_dot = jnp.sum(probs * grad_probs, axis=0, keepdims=True)
        grad_scores = (probs * (grad_probs - row_dot)).astype(jnp.bfloat16)
        grad_keys = jnp.dot(grad_scores, queries, preferred_element_type=jnp.float32)
        grad_queries = row_outer(keys, grad_scores) * scale
        qs[h, :, 0:HD] = grad_queries.T.astype(jnp.bfloat16)
        ks[h, :, 0:HD] = (grad_keys * scale).astype(jnp.bfloat16)
        vs[h, :, 0:HD] = grad_values.astype(jnp.bfloat16)
        return carry

    lax.fori_loop(0, HEADS, one_head, 0, unroll=4)
    side_by_side(qs, 0, tokens, dq_ref, 0)
    side_by_side(ks, 0, tokens, near_ref, 0)
    side_by_side(vs, 0, tokens, near_ref, D)
    side_by_side(ks, tokens, tokens, far_ref, 0)
    side_by_side(vs, tokens, tokens, far_ref, D)


def attend_back_pair(own, other, grad):
    tokens = own.shape[0]
    return pl.pallas_call(
        attend_back_kernel,
        out_shape=(
            jax.ShapeDtypeStruct((tokens, D), jnp.bfloat16),
            jax.ShapeDtypeStruct((tokens, 2 * D), jnp.bfloat16),
            jax.ShapeDtypeStruct((tokens, 2 * D), jnp.bfloat16),
        ),
        scratch_shapes=[
            pltpu.VMEM((HEADS, tokens, 128), jnp.bfloat16),
            pltpu.VMEM((HEADS, tokens, 128), jnp.bfloat16),
            pltpu.VMEM((HEADS, 2 * tokens, 128), jnp.bfloat16),
            pltpu.VMEM((HEADS, 2 * tokens, 128), jnp.bfloat16),
        ],
        compiler_params=pltpu.CompilerParams(vmem_limit_bytes=56 * 2**20),
        cost_estimate=pl.CostEstimate(
            flops=182 * tokens * tokens * D, bytes_accessed=22 * tokens * D, transcendentals=0
        ),
    )(own, other, grad)


def units_first(weight, units):
    rows = weight.reshape(UNIT, units, D)
    return jnp.swapaxes(rows, 0, 1).reshape(units * UNIT, D)


def units_last(shard, units):
    rows = shard.reshape(units, UNIT, D)
    return jnp.swapaxes(rows, 0, 1).reshape(-1)


def per_device_paired(
    latents,
    conditions,
    cotangent,
    qkv_weight,
    proj_weight,
    fc1_weight,
    fc2_weight,
    ada_weight,
    biases,
    qkv_first,
    proj_first,
    fc1_first,
    fc2_first,
    ada_first,
    bias_first,
    qkv_second,
    proj_second,
    fc1_second,
    fc2_second,
    ada_second,
    bias_second,
):
    tokens = latents.shape[1]
    me = flat_index()
    y, core = me % 2, (me // 2) % 2
    latent = (me // 4) * 2 + y

    shard_attention = jnp.concatenate(
        [
            units_first(qkv_weight.astype(jnp.bfloat16), 3),
            units_first(proj_weight.astype(jnp.bfloat16), 1),
        ],
        axis=0,
    )
    shard_fc1 = units_first(fc1_weight.astype(jnp.bfloat16), 4)
    shard_fc2 = fc2_weight.astype(jnp.bfloat16).reshape(ROWS, D)
    line_attention = gather_line(shard_attention)
    line_mlp = gather_line(after(jnp.stack([shard_fc1, shard_fc2]), line_attention))

    latents_here, cotangent_here = relocate(latents), relocate(cotangent)
    silu_low = silu_apply(conditions).astype(jnp.bfloat16)
    all_silu = lax.all_to_all(
        jnp.broadcast_to(silu_low, (16, D)), "dp", 0, 0, tiled=True
    )
    ada_low = ada_weight.astype(jnp.bfloat16)
    ada_rows, bias_count = ada_low.shape[0], biases.shape[0]
    own_rows = times_transposed(all_silu, ada_low)
    by_device = jnp.broadcast_to(
        own_rows.reshape(8, 1, 2, ada_rows), (8, 2, 2, ada_rows)
    ).reshape(DEVICES, ada_rows)
    small = exchange(
        jnp.concatenate(
            [
                by_device,
                jnp.broadcast_to(biases[None], (DEVICES, bias_count)),
                jnp.zeros((DEVICES, 48), jnp.float32),
            ],
            axis=1,
        )
    )
    bias_all = small[:, ada_rows : ada_rows + bias_count].reshape(-1)
    modulation = small[:, :ada_rows].reshape(6, D) + bias_all[4 * D + MLP :].reshape(6, D)
    shift_attn, scale_attn, gate_attn, shift_mlp, scale_mlp, gate_mlp = (
        modulation[i : i + 1] for i in range(6)
    )

    line_attention, latents_here, cotangent_here = all_after(
        (line_attention, latents_here, cotangent_here), small
    )
    inputs = latents_here.reshape(tokens, D).astype(jnp.float32)
    grad_out = cotangent_here.reshape(tokens, D).astype(jnp.float32)

    own_attention = column_parts(line_attention)
    first_attention = widen(own_attention, swap_parts(own_attention, FIRST_BITS))
    second_attention = swap_parts(first_attention, SECOND_BITS)
    w_qkv, w_proj = assemble(gather_cores(first_attention, second_attention), "attention")
    line_mlp = after(line_mlp, *second_attention)
    own_fc1 = column_parts(line_mlp[:, 0])
    first_fc1 = all_after(widen(own_fc1, swap_parts(own_fc1, FIRST_BITS)), w_qkv)
    second_fc1 = swap_parts(first_fc1, SECOND_BITS)
    own_fc2 = column_parts(after(line_mlp, *first_fc1)[:, 1])

    normed_a, inv_std_a = layer_norm(inputs)
    hidden_a = (normed_a * (1.0 + scale_attn) + shift_attn).astype(jnp.bfloat16)
    bias_qkv = jnp.concatenate([bias_all[:D], jnp.zeros((D,), jnp.float32), bias_all[D : 2 * D]])
    qkv_low = (jnp.dot(after(hidden_a, *first_fc1, *own_fc2), w_qkv, preferred_element_type=jnp.float32) + bias_qkv).astype(
        jnp.bfloat16
    )
    other = swap(qkv_low[:, D:], CORE_BIT)
    near_fc2 = swap_parts(own_fc2, FIRST_BITS)
    attended_low = attend(qkv_low, other)
    first_fc2 = widen(all_after(own_fc2, attended_low), near_fc2)
    second_fc2 = swap_parts(first_fc2, SECOND_BITS)
    (w_fc1,) = assemble(
        gather_cores(
            all_after(first_fc1, attended_low), all_after(second_fc1, attended_low)
        ),
        "fc1",
    )
    branch_a = (
        jnp.dot(attended_low, w_proj, preferred_element_type=jnp.float32) + bias_all[2 * D : 3 * D]
    )
    middle = inputs + gate_attn * branch_a
    normed_m, inv_std_m = layer_norm(middle)
    hidden_m = (normed_m * (1.0 + scale_mlp) + shift_mlp).astype(jnp.bfloat16)
    pre_act = (
        jnp.dot(after(hidden_m, *first_fc2), w_fc1, preferred_element_type=jnp.float32) + bias_all[3 * D : 3 * D + MLP]
    )
    act_low = gelu_apply(pre_act).astype(jnp.bfloat16)
    grad_branch_m = (gate_mlp * grad_out).astype(jnp.bfloat16)
    grad_fc2 = row_outer(act_low, grad_branch_m).astype(jnp.bfloat16)
    halves_fc2 = split_core((after(grad_fc2, *second_fc2),), "fc2")
    pieces_fc2 = gather_cores(
        all_after(first_fc2, grad_fc2), all_after(second_fc2, grad_fc2)
    )
    halves_fc2 = all_after(halves_fc2, *pieces_fc2[0], *pieces_fc2[1])
    (w_fc2,) = assemble(pieces_fc2, "fc2")
    half_fc2 = scatter_cores(*halves_fc2)
    branch_m = (
        jnp.dot(act_low, w_fc2, preferred_element_type=jnp.float32)
        + bias_all[3 * D + MLP : 4 * D + MLP]
    )
    block_out = relocate((middle + gate_mlp * branch_m).astype(jnp.bfloat16))[None]
    grad_gate_m = jnp.sum(grad_out * branch_m, axis=0)
    grad_b2 = jnp.sum(grad_branch_m.astype(jnp.float32), axis=0)
    grad_act = times_transposed(after(grad_branch_m, *halves_fc2), w_fc2)
    gelu_pull = jax.vjp(gelu_apply, pre_act)[1]
    grad_pre = gelu_pull(grad_act)[0].astype(jnp.bfloat16)
    keeps, sends = first_halves(half_fc2)
    grad_fc1 = row_outer(after(hidden_m, *sends), grad_pre).astype(jnp.bfloat16)
    first_grad_fc2 = add_parts(keeps, swap_parts(sends, SECOND_BITS))
    halves_fc1 = split_core((grad_fc1,), "fc1")
    half_fc1 = scatter_cores(*halves_fc1)
    grad_b1 = jnp.sum(grad_pre.astype(jnp.float32), axis=0)
    grad_hidden_m = times_transposed(after(grad_pre, *halves_fc1), w_fc1)
    grad_scale_m = jnp.sum(grad_hidden_m * normed_m, axis=0)
    grad_shift_m = jnp.sum(grad_hidden_m, axis=0)
    grad_middle = grad_out + norm_back(grad_hidden_m * (1.0 + scale_mlp), normed_m, inv_std_m)
    grad_gate_a = jnp.sum(grad_middle * branch_a, axis=0)
    grad_branch_a = (gate_attn * grad_middle).astype(jnp.bfloat16)
    grad_proj = row_outer(attended_low, grad_branch_a).astype(jnp.bfloat16)
    grad_bproj = jnp.sum(grad_branch_a.astype(jnp.float32), axis=0)
    grad_att = times_transposed(grad_branch_a, w_proj).astype(jnp.bfloat16)
    keeps_fc2, sends_fc2 = second_halves(first_grad_fc2)
    keeps_fc1, sends_fc1 = first_halves(half_fc1)
    grad_att = after(grad_att, *sends_fc2, *sends_fc1)
    others_fc2 = swap_parts(sends_fc2, FIRST_BITS)
    others_fc1 = swap_parts(sends_fc1, SECOND_BITS)
    grad_queries, near, far = attend_back_pair(qkv_low, other, grad_att)
    second_grad_fc2 = add_parts(all_after(keeps_fc2, grad_queries), others_fc2)
    first_grad_fc1 = add_parts(all_after(keeps_fc1, grad_queries), others_fc1)
    keeps_fc1, sends_fc1 = second_halves(first_grad_fc1)
    far = after(far, *others_fc2, *others_fc1)
    grad_qkv = jnp.concatenate([grad_queries, add_low(near, swap(far, CORE_BIT))], axis=-1)
    late_hidden = after(hidden_a, *second_grad_fc2, *sends_fc1)
    summed_fc2 = scatter_line(second_grad_fc2)
    summed_fc1 = scatter_line(add_parts(keeps_fc1, swap_parts(sends_fc1, FIRST_BITS)))
    grad_wqkv = row_outer(late_hidden, grad_qkv).astype(jnp.bfloat16)
    halves_attention = split_core((grad_wqkv, grad_proj), "attention")
    half_attention = scatter_cores(*halves_attention)
    keeps_attention, sends_attention = first_halves(half_attention)
    sums_qkv = jnp.sum(grad_qkv.astype(jnp.float32), axis=0)
    grad_hidden_a = times_transposed(after(grad_qkv, *halves_attention), w_qkv)
    grad_scale_a = jnp.sum(grad_hidden_a * normed_a, axis=0)
    grad_shift_a = jnp.sum(grad_hidden_a, axis=0)
    input_grad = grad_middle + norm_back(grad_hidden_a * (1.0 + scale_attn), normed_a, inv_std_a)

    grad_mod = jnp.concatenate(
        [grad_shift_a, grad_scale_a, grad_gate_a, grad_shift_m, grad_scale_m, grad_gate_m]
    )
    grad_bias = jnp.concatenate(
        [sums_qkv[:D], sums_qkv[2 * D :], grad_bproj, grad_b1, grad_b2, grad_mod]
    )
    payload = jnp.concatenate(
        [
            grad_mod.reshape(DEVICES, -1),
            grad_bias.reshape(DEVICES, -1),
            jnp.zeros((DEVICES, 48), jnp.float32),
        ],
        axis=1,
    )
    received = exchange(after(payload, *sends_attention))
    first_grad_attention = add_parts(
        all_after(keeps_attention, received), swap_parts(sends_attention, SECOND_BITS)
    )
    keeps_attention, sends_attention = second_halves(first_grad_attention)
    grad_rows = jnp.sum(received[:, :ada_rows].reshape(8, 2, 2, ada_rows), axis=1).reshape(
        16, ada_rows
    )
    summed_bias = jnp.sum(received[:, ada_rows : ada_rows + bias_count], axis=0)
    summed_ada = jnp.dot(grad_rows.T, all_silu.astype(jnp.float32), precision=lax.Precision.HIGHEST)
    silu_terms = jnp.dot(grad_rows, ada_low.astype(jnp.float32), precision=lax.Precision.HIGHEST)
    silu_terms = jnp.broadcast_to(silu_terms[:, None, :], (16, 2, D)).reshape(DEVICES, D)
    silu_parts = exchange(after(silu_terms, *sends_attention))
    line_parts = add_parts(
        all_after(keeps_attention, silu_terms), swap_parts(sends_attention, FIRST_BITS)
    )
    summed_attention = scatter_line(line_parts)
    moved_grad = relocate(after(input_grad.astype(jnp.bfloat16), *line_parts))
    input_grad = jnp.where(y == core, input_grad, moved_grad.astype(jnp.float32))[None]
    grad_silu = jnp.sum(silu_parts, axis=0, keepdims=True)
    silu_pull = jax.vjp(silu_apply, conditions)[1]
    cond_grad = silu_pull(grad_silu)[0]

    rate_wide = 2.0 * D ** (-0.5)
    rate_proj = 2.0 * max(1, D * 256 // TOK_MIN) ** (-0.5)
    rate_fc2 = 2.0 * MLP ** (-0.5)
    summed_qkv = units_last(summed_attention[: 3 * UNIT], 3)
    summed_proj = summed_attention[3 * UNIT :].reshape(-1)
    new_qkv, qkv_m, qkv_s = adamw_update(qkv_weight, qkv_first, qkv_second, summed_qkv, rate_wide)
    new_proj, proj_m, proj_s = adamw_update(
        proj_weight, proj_first, proj_second, summed_proj, rate_proj
    )
    new_fc1, fc1_m, fc1_s = adamw_update(
        fc1_weight, fc1_first, fc1_second, units_last(summed_fc1, 4), rate_wide
    )
    new_fc2, fc2_m, fc2_s = adamw_update(
        fc2_weight, fc2_first, fc2_second, summed_fc2.reshape(-1), rate_fc2
    )
    new_ada, ada_m, ada_s = adamw_update(ada_weight, ada_first, ada_second, summed_ada, rate_wide)
    new_bias, bias_m, bias_s = adamw_update(biases, bias_first, bias_second, summed_bias, 0.6)
    return (
        block_out,
        input_grad,
        cond_grad,
        new_qkv,
        new_proj,
        new_fc1,
        new_fc2,
        new_ada,
        new_bias,
        qkv_m,
        proj_m,
        fc1_m,
        fc2_m,
        ada_m,
        bias_m,
        qkv_s,
        proj_s,
        fc1_s,
        fc2_s,
        ada_s,
        bias_s,
    )


def solution(mesh):
    in_specs = (
        P("dp", "seq", None),
        P("dp", None),
        P("dp", "seq", None),
        P(("dp", "seq")),
        P(("dp", "seq")),
        P(("dp", "seq")),
        P(("dp", "seq")),
        P(("dp", "seq"), None),
        P(("dp", "seq")),
        P(("dp", "seq")),
        P(("dp", "seq")),
        P(("dp", "seq")),
        P(("dp", "seq")),
        P(("dp", "seq"), None),
        P(("dp", "seq")),
        P(("dp", "seq")),
        P(("dp", "seq")),
        P(("dp", "seq")),
        P(("dp", "seq")),
        P(("dp", "seq"), None),
        P(("dp", "seq")),
    )
    out_specs = (
        P("dp", "seq", None),
        P("dp", "seq", None),
        P("dp", None),
        P(("dp", "seq")),
        P(("dp", "seq")),
        P(("dp", "seq")),
        P(("dp", "seq")),
        P(("dp", "seq"), None),
        P(("dp", "seq")),
        P(("dp", "seq")),
        P(("dp", "seq")),
        P(("dp", "seq")),
        P(("dp", "seq")),
        P(("dp", "seq"), None),
        P(("dp", "seq")),
        P(("dp", "seq")),
        P(("dp", "seq")),
        P(("dp", "seq")),
        P(("dp", "seq")),
        P(("dp", "seq"), None),
        P(("dp", "seq")),
    )
    eight = mesh.shape["dp"] == 16 and mesh.shape["seq"] == 2
    return jax.shard_map(
        per_device_paired if eight else per_device, mesh=mesh, in_specs=in_specs, out_specs=out_specs, check_vma=False
    )
```
